32 devices in a mesh: visit: 4 (over y, x), patch: 8 (over z, core).
Axes of the slice: x: 2, y: 2, z: 4, core: 2. Of those that a mesh axis runs over, the one named last changes fastest.
Arguments:
- image: float32 [4, 8, 32, 128, 128], P('visit', 'patch'), may hold values from -6 to 6
- variance: float32 [4, 8, 32, 128, 128], P('visit', 'patch'), may hold values from 4 to 64
- dest_patch: int32 [4, 8, 32], P('visit', 'patch'), may hold values from 0 to 7, as said below
- quadrant: int32 [4, 8, 32], P('visit', 'patch'), may hold values from 0 to 3
- coef_index: int32 [4, 8, 32], P('visit', 'patch'), may hold values from 0 to 799
- block_count: int32 [4, 8], P('visit', 'patch'), may hold values from 24 to 32, as said below
- coef_table: float32 [800, 16, 6], replicated, may hold values from -0.625 to 0.625
- row_taps: float32 [16, 41], replicated, may hold values from -1 to 1
- col_taps: float32 [16, 41], replicated, may hold values from -1 to 1
Outputs:
- weighted_sum: float32 [8, 256, 256], P('patch', 'visit')
- weight_sum: float32 [8, 256, 256], P('patch', 'visit')
The draws below stay inside these ranges and needn't reach their ends.
Inputs may be any that keep to these rules, and one draw needn't show every extreme that they name: `dest_patch`: among the blocks of one device at most 8 name the same patch slice; one patch slice, drawn from the seed, is named by exactly 8 live blocks of every device. `block_count`: some device has all 32 blocks live.
All inputs are finite; a program needn't handle non-finite values.
Results may differ from the reference program's by a relative error of at most 0.0003.
Values sent between devices are 32-bit elements; how exact they have to be, the bound alone decides.
No kernel may reach another device: no remote copies, remote signals or barrier semaphores. Data moves between devices by JAX's collectives and lax.ppermute only.
A program may use at most 192 MiB of HBM per device.

```python
import math
import jax
import jax.numpy as jnp
from jax import lax

BLOCK = 128
BLK_DEV = 32
TAPS = 41
NBASIS = 16
NPOLY = 6
NTAB = 800
CAP = 8
N_VISIT = 4
N_PATCH = 8


def draw_dest_patch(key, part):
    slot_total = N_PATCH * CAP
    key_heavy, key_favour, key_score, key_order = jax.random.split(key, 4)
    heavy_owner = jax.random.randint(key_heavy, (), 0, N_PATCH)
    favour = jax.random.randint(key_favour, (N_PATCH,), 1, 5)
    slot_owner = jnp.arange(slot_total) // CAP
    random_part = jax.random.randint(key_score, (N_VISIT, N_PATCH, slot_total), 0, 1000)
    slot_score = random_part * favour[slot_owner][None, None, :] + 5000 * (slot_owner == heavy_owner).astype(jnp.int32)[None, None, :]
    slot_score = slot_score * slot_total + jnp.arange(slot_total)[None, None, :]
    best_score, chosen = lax.top_k(slot_score, BLK_DEV)
    targets = chosen // CAP
    live_front = 3 * BLK_DEV // 4
    position = jnp.arange(BLK_DEV)
    shuffle = jax.random.randint(key_order, (N_VISIT, N_PATCH, BLK_DEV), 0, 1 << 20)
    sort_key = jnp.where(position[None, None, :] < live_front, shuffle * BLK_DEV + position[None, None, :], (1 << 20) * BLK_DEV + position[None, None, :])
    placing = jnp.argsort(sort_key, axis=-1, stable=True)
    return jnp.take_along_axis(targets, placing, axis=-1).astype(jnp.int32)


def draw_block_count(key, part):
    key_counts, key_full = jax.random.split(key)
    live_counts = jax.random.randint(key_counts, (N_VISIT, N_PATCH), 3 * BLK_DEV // 4, BLK_DEV + 1)
    full_cell = jax.random.randint(key_full, (), 0, N_VISIT * N_PATCH)
    flat_counts = jnp.where(jnp.arange(N_VISIT * N_PATCH) == full_cell, BLK_DEV, live_counts.reshape(-1))
    return flat_counts.reshape(N_VISIT, N_PATCH).astype(jnp.int32)


def place_ends(values, own_key, least, high):
    extent = values.shape
    index_at = [jax.random.randint(jax.random.fold_in(own_key, axis), (), 0, extent[axis]) for axis in range(len(extent))]
    values = values.at[tuple(index_at)].set(least)
    longest = extent.index(max(extent))
    index_at[longest] = (index_at[longest] + 1) % extent[longest]
    return values.at[tuple(index_at)].set(high)


def steps_of(own_key, shape, pieces, low, top_value):
    def one(dim, shards_of):
        heights = jax.random.uniform(jax.random.fold_in(jax.random.fold_in(own_key, 6), dim), (shards_of,), jnp.float32, low / len(pieces), top_value / len(pieces))
        return jnp.repeat(jnp.exp(heights), shape[dim] // shards_of).reshape((-1,) + (1,) * (len(shape) - dim - 1))

    factor_of = one(*pieces[0])
    for cut in pieces[1:]:
        factor_of = factor_of * one(*cut)
    return factor_of


def bell_draw(key, shape, deviation, reach, cuts=(), dtype=jnp.bfloat16):
    loudness = steps_of(key, shape, cuts, -0.22, 0.18) if cuts else 1.0
    result = jax.random.normal(key, shape, jnp.float32) * deviation * loudness
    return jnp.minimum(jnp.maximum(result, -reach), reach).astype(dtype)


def setup_inputs(seed: int = 0) -> dict:
    key_of = jax.random.split(jax.random.key(seed), 10)
    image = bell_draw(key_of[0], (N_VISIT, N_PATCH, BLK_DEV, BLOCK, BLOCK), 1.0, 6.0, ((0, 4), (1, 8)), jnp.float32)
    variance = jnp.clip(jnp.exp(math.log(64.0) - 2.7725887 * jax.random.uniform(key_of[1], (N_VISIT, N_PATCH, BLK_DEV, BLOCK, BLOCK), jnp.float32) ** steps_of(key_of[1], (N_VISIT, N_PATCH, BLK_DEV, BLOCK, BLOCK), ((0, 4), (1, 8)), -0.2, 0.2)), 4.0, 64.0)
    dest_patch = draw_dest_patch(jax.random.fold_in(key_of[9], 71), 0)
    quadrant = place_ends(jax.random.randint(key_of[3], (N_VISIT, N_PATCH, BLK_DEV), 0, 4), jax.random.fold_in(key_of[3], 1), 0, 3).astype(jnp.int32)
    coef_index = place_ends(jax.random.randint(key_of[4], (N_VISIT, N_PATCH, BLK_DEV), 0, NTAB), jax.random.fold_in(key_of[4], 1), 0, NTAB - 1).astype(jnp.int32)
    block_count = draw_block_count(jax.random.fold_in(key_of[9], 71), 0)
    coef_table = bell_draw(key_of[6], (NTAB, NBASIS, NPOLY), (NBASIS * NPOLY) ** -0.5, 0.625, (), jnp.float32)
    row_taps = bell_draw(key_of[7], (NBASIS, TAPS), TAPS ** -0.5, 1.0, (), jnp.float32)
    col_taps = bell_draw(key_of[8], (NBASIS, TAPS), TAPS ** -0.5, 1.0, (), jnp.float32)
    return {"image": image, "variance": variance, "dest_patch": dest_patch, "quadrant": quadrant, "coef_index": coef_index, "block_count": block_count, "coef_table": coef_table, "row_taps": row_taps, "col_taps": col_taps}


highest = lax.Precision.HIGHEST


def band_matrices(filter_taps, block_side, reversed_band):
    radius = (filter_taps.shape[1] - 1) // 2
    row_index = jnp.arange(block_side)[:, None]
    col_index = jnp.arange(block_side)[None, :]
    offset = row_index - col_index if reversed_band else col_index - row_index
    banded = jnp.zeros((filter_taps.shape[0], block_side, block_side), jnp.float32)
    for tap_index in range(filter_taps.shape[1]):
        picked = (offset == tap_index - radius).astype(jnp.float32)
        banded = banded + filter_taps[:, tap_index, None, None] * picked[None, :, :]
    return banded


def match_blocks(pixels, coefficients, down_quarter, across_quarter, row_band, col_band):
    block_side = pixels.shape[-1]
    pixel_index = jnp.arange(block_side).astype(jnp.float32)
    across_pos = ((across_quarter[:, None] * block_side + pixel_index[None, :]) + 0.5) / block_side - 1.0
    down_pos = ((down_quarter[:, None] * block_side + pixel_index[None, :]) + 0.5) / block_side - 1.0
    across_pos = across_pos[:, None, :]
    down_pos = down_pos[:, :, None]
    matched = jnp.zeros(pixels.shape, jnp.float32)
    for basis_index in range(row_band.shape[0]):
        spread = jnp.einsum("nij,jk->nik", pixels, row_band[basis_index], precision=highest, preferred_element_type=jnp.float32)
        convolved = jnp.einsum("ij,njk->nik", col_band[basis_index], spread, precision=highest, preferred_element_type=jnp.float32)
        poly_terms = coefficients[:, basis_index, :]
        weight = (poly_terms[:, 0, None, None] + poly_terms[:, 1, None, None] * across_pos
                  + poly_terms[:, 2, None, None] * down_pos + poly_terms[:, 3, None, None] * across_pos * across_pos
                  + poly_terms[:, 4, None, None] * across_pos * down_pos + poly_terms[:, 5, None, None] * down_pos * down_pos)
        matched = matched + weight * convolved
    return matched


def reference(image, variance, dest_patch, quadrant, coef_index, block_count, coef_table, row_taps, col_taps):
    block_side = image.shape[-1]
    row_band = band_matrices(row_taps, block_side, False)
    col_band = band_matrices(col_taps, block_side, True)
    devices_all = image.shape[0] * image.shape[1]
    blocks = image.shape[2]
    live_mask = jnp.arange(blocks)[None, None, :] < block_count[:, :, None]
    stacked = (image.reshape(devices_all, blocks, block_side, block_side),
               variance.reshape(devices_all, blocks, block_side, block_side),
               dest_patch.reshape(devices_all, blocks).astype(jnp.int32),
               quadrant.reshape(devices_all, blocks).astype(jnp.int32),
               coef_index.reshape(devices_all, blocks).astype(jnp.int32),
               live_mask.reshape(devices_all, blocks))
    start = (jnp.zeros((N_PATCH, 2, block_side, 2, block_side), jnp.float32),
             jnp.zeros((N_PATCH, 2, block_side, 2, block_side), jnp.float32))

    def add_device(running, device_item):
        weighted, weight_total = running
        pixels, variances, targets, quadrants, table_rows, is_live = device_item
        down_quarter = (quadrants // 2).astype(jnp.float32)
        across_quarter = (quadrants % 2).astype(jnp.float32)
        matched = match_blocks(pixels, coef_table[table_rows], down_quarter, across_quarter, row_band, col_band)
        inverse = is_live.astype(jnp.float32)[:, None, None] / variances
        weighted = weighted.at[targets, quadrants // 2, :, quadrants % 2, :].add(inverse * matched)
        weight_total = weight_total.at[targets, quadrants // 2, :, quadrants % 2, :].add(inverse)
        return (weighted, weight_total), None

    (weighted, weight_total), unused = lax.scan(add_device, start, stacked)
    return (weighted.reshape(N_PATCH, 2 * block_side, 2 * block_side),
            weight_total.reshape(N_PATCH, 2 * block_side, 2 * block_side))
```

```python
import functools

import jax
import jax.numpy as jnp
from jax import lax
from jax.experimental import pallas as pl
from jax.experimental.pallas import tpu as pltpu
from jax.sharding import PartitionSpec as P

f32 = jnp.float32
bf16 = jnp.bfloat16

SHARE = 1.0 / 32.0
KEEP = 1.0 - SHARE
VMEM_BYTES = 40 * 2**20


def split_left(value):
    first = value.astype(bf16)
    return first, (value - KEEP * first.astype(f32)).astype(bf16)


def split_right(value):
    first = (KEEP * value).astype(bf16)
    return first, ((value - first.astype(f32)) * (1.0 / SHARE)).astype(bf16)


def place_of(where, target, quarter):
    core = lax.rem(target, 2) ^ where[0]
    depth = lax.rem(target // 2 - where[1] + where[2], where[2])
    return core, depth, (quarter // 2) ^ where[3], lax.rem(quarter, 2)


def prepare_kernel(
    where, targets, quarters, count, variance, row_taps, col_taps,
    keep_out, send_out, col_band, row_band, canvas, padded,
):
    blocks, side, _ = variance.shape
    half = side // 2
    nbasis, taps = row_taps.shape
    radius = (taps - 1) // 2
    canvas[...] = jnp.zeros_like(canvas)

    def add_block(n, carry):
        live = jnp.where(n < count[0], 1.0, 0.0).astype(f32)
        inverse = live / variance[n]
        core, depth, down, across = place_of(where, targets[n], quarters[n])
        column = pl.ds(pl.multiple_of(across * side, side), side)
        for part in range(2):
            canvas[core, part ^ where[4], down, depth, :, column] += inverse[
                part * half : (part + 1) * half
            ]
        return carry

    lax.fori_loop(0, blocks, add_block, 0)
    keep_out[...] = canvas[0]
    send_out[...] = canvas[1]

    row = lax.broadcasted_iota(jnp.int32, (side, side), 0)
    column = lax.broadcasted_iota(jnp.int32, (side, side), 1)
    near = jnp.abs(row - column) <= radius
    padded[...] = jnp.zeros_like(padded)
    padded[:, :taps] = row_taps[...]
    row_placed = pltpu.roll(padded[...], side - radius, 1)
    padded[:, :taps] = col_taps[...]
    turn = (lax.rem(column - radius + row + side, side) == 0).astype(f32)
    col_placed = jnp.dot(
        padded[...], turn, precision=lax.Precision.HIGHEST, preferred_element_type=f32
    )
    for k in range(nbasis):
        base = jnp.broadcast_to(row_placed[k : k + 1], (side, side))
        band = jnp.where(near, pltpu.roll(base, 0, 1, stride=1, stride_axis=0), 0.0)
        first, second = split_right(band)
        row_band[k, :side, :] = first
        row_band[k, side:, :] = second
        base = jnp.broadcast_to(col_placed[k : k + 1], (side, side))
        band = jnp.where(near, pltpu.roll(base, 0, 1, stride=1, stride_axis=0), 0.0)
        first, second = split_left(band)
        col_band[k, :, :side] = first
        col_band[k, :, side:] = second


def prepare(where, targets, quarters, count, variance, row_taps, col_taps, depths):
    blocks, side, _ = variance.shape
    nbasis = row_taps.shape[0]
    half = side // 2
    part = jax.ShapeDtypeStruct((2, 2, depths, half, 2 * side), f32)
    scalar = pl.BlockSpec(memory_space=pltpu.SMEM)
    vector = pl.BlockSpec(memory_space=pltpu.VMEM)
    return pl.pallas_call(
        prepare_kernel,
        out_shape=(
            part,
            part,
            jax.ShapeDtypeStruct((nbasis, side, 2 * side), bf16),
            jax.ShapeDtypeStruct((nbasis, 2 * side, side), bf16),
        ),
        in_specs=[scalar] * 4 + [vector] * 3,
        out_specs=[vector] * 4,
        scratch_shapes=[
            pltpu.VMEM((2, 2, 2, depths, half, 2 * side), f32),
            pltpu.VMEM((nbasis, side), f32),
        ],
        compiler_params=pltpu.CompilerParams(vmem_limit_bytes=VMEM_BYTES),
        cost_estimate=pl.CostEstimate(flops=10**7, bytes_accessed=10**7, transcendentals=0),
    )(where, targets, quarters, count, variance, row_taps, col_taps)


def match_kernel(
    first_row, where, targets, quarters, table_rows, count, pixels, variance, table,
    col_band, row_band, keep_out, send_out, canvas, total, coefficients,
):
    blocks, side, _ = pixels.shape
    nbasis = col_band.shape[0]
    rows = canvas.shape[3]
    group = total.shape[0]
    top = pl.multiple_of(first_row[0], rows)
    canvas[...] = jnp.zeros_like(canvas)
    entries = table.shape[2]
    coefficients[:, :, :entries] = table[...]
    lane = lax.broadcasted_iota(jnp.int32, (1, side), 1).astype(f32)
    sub = lax.broadcasted_iota(jnp.int32, (8, side), 0).astype(f32)
    step = 8.0 / side
    left = col_band[:, pl.ds(top, rows), :].reshape(nbasis * rows, 2 * side)

    def add_group(j, carry):
        terms = []
        for member in range(group):
            n = group * j + member
            quarter = quarters[n]
            across = (lane + 0.5) / side - 1.0 + lax.rem(quarter, 2).astype(f32)
            down = (sub + 0.5 + top.astype(f32)) / side - 1.0 + (quarter // 2).astype(f32)
            entry = table_rows[n]
            chunk = coefficients[:, :, pl.ds(pl.multiple_of((entry // 128) * 128, 128), 128)]
            chunk = chunk.reshape(-1, 128)
            chunk = pltpu.roll(chunk, lax.rem(128 - lax.rem(entry, 128), 128), 1)
            poly = jnp.broadcast_to(chunk[:, :1], (chunk.shape[0], side))
            poly = [poly[i * nbasis : (i + 1) * nbasis] for i in range(chunk.shape[0] // nbasis)]
            constant = poly[0] + across * (poly[1] + across * poly[3])
            linear = poly[2] + across * poly[4]
            terms.append((constant, linear, poly[5], down))
        halves = []
        for pair in range(group // 2):
            n = group * j + 2 * pair
            both = jnp.concatenate([pixels[n], pixels[n + 1]], axis=1)
            right = jnp.concatenate(split_right(both), axis=0)
            convolved = jnp.dot(left, right, preferred_element_type=f32)
            halves.append(split_left(convolved))
        for k in range(nbasis):
            at = slice(k * rows, (k + 1) * rows)
            stacked = []
            for member in range(group):
                first, second = halves[member // 2]
                lanes = slice((member % 2) * side, (member % 2 + 1) * side)
                stacked.append(jnp.concatenate([first[at, lanes], second[at, lanes]], axis=1))
            spread = jnp.dot(
                jnp.concatenate(stacked, axis=0), row_band[k], preferred_element_type=f32
            )
            for member in range(group):
                constant, linear, square, down = terms[member]
                b, d = linear[k : k + 1], square[k : k + 1]
                weight = constant[k : k + 1] + down * (b + down * d)
                change = step * b + d * (2.0 * step * down + step * step)
                second_change = (2.0 * step * step) * d
                for i in range(rows // 8):
                    value = weight * spread[member * rows + 8 * i : member * rows + 8 * i + 8]
                    if k == 0:
                        total[member, 8 * i : 8 * i + 8] = value
                    else:
                        total[member, 8 * i : 8 * i + 8] += value
                    if i < rows // 8 - 1:
                        weight = weight + change
                        change = change + second_change
        for member in range(group):
            n = group * j + member
            live = jnp.where(n < count[0], 1.0, 0.0).astype(f32)
            core, depth, down, across = place_of(where, targets[n], quarters[n])
            column = pl.ds(pl.multiple_of(across * side, side), side)
            canvas[core, down, depth, :, column] += (
                live / variance[n, pl.ds(top, rows), :]
            ) * total[member]
        return carry

    lax.fori_loop(0, blocks // group, add_group, 0)
    keep_out[...] = canvas[0]
    send_out[...] = canvas[1]


def match(
    first_row, rows, where, targets, quarters, table_rows, count, pixels, variance, table,
    col_band, row_band, depths,
):
    blocks, side, _ = pixels.shape
    group = min(blocks, 256 // rows)
    part = jax.ShapeDtypeStruct((2, depths, rows, 2 * side), f32)
    scalar = pl.BlockSpec(memory_space=pltpu.SMEM)
    vector = pl.BlockSpec(memory_space=pltpu.VMEM)
    entries = -(-table.shape[2] // 128) * 128
    return pl.pallas_call(
        match_kernel,
        out_shape=(part, part),
        in_specs=[scalar] * 6 + [vector] * 5,
        out_specs=[vector] * 2,
        scratch_shapes=[
            pltpu.VMEM((2, 2, depths, rows, 2 * side), f32),
            pltpu.VMEM((group, rows, side), f32),
            pltpu.VMEM(table.shape[:2] + (entries,), f32),
        ],
        compiler_params=pltpu.CompilerParams(vmem_limit_bytes=VMEM_BYTES),
        cost_estimate=pl.CostEstimate(
            flops=2 * blocks * rows * side * 20 * 512, bytes_accessed=10**7, transcendentals=0
        ),
    )(
        first_row, where, targets, quarters, table_rows, count, pixels, variance, table,
        col_band, row_band,
    )


def on_device(
    image, variance, dest_patch, quadrant, coef_index, block_count, coef_table, row_taps, col_taps
):
    pixels = image[0, 0]
    variances = variance[0, 0]
    targets = dest_patch[0, 0]
    quarters = quadrant[0, 0]
    table_rows = coef_index[0, 0]
    count = block_count[0]
    owners = lax.axis_size("patch")
    visits = lax.axis_size("visit")
    depths = owners // 2
    half = pixels.shape[1] // 2
    patch_at = lax.axis_index("patch")
    visit_at = lax.axis_index("visit")
    my_x = lax.rem(visit_at, 2)
    where = jnp.stack(
        [lax.rem(patch_at, 2), patch_at // 2, jnp.int32(depths), visit_at // 2, my_x]
    ).astype(jnp.int32)
    table = jnp.transpose(coef_table, (2, 1, 0))

    def over_core(value):
        return lax.ppermute(value, "patch", [(i, i ^ 1) for i in range(owners)])

    def over_visit(value, flip):
        return lax.ppermute(value, "visit", [(i, i ^ flip) for i in range(visits)])

    def over_depth(value, shift):
        return lax.ppermute(
            value, "patch", [(i, (i + 2 * shift) % owners) for i in range(owners)]
        )

    def finish(value):
        pieces = [over_depth(value[s], s) for s in range(1, depths)]
        return functools.reduce(jnp.add, pieces, value[0])

    keep, send, col_band, row_band = prepare(
        where, targets, quarters, count, variances, row_taps, col_taps, depths
    )
    got = over_core(send)
    mine = {}
    for x in range(2):
        for y in range(2):
            mine[x, y] = keep[x, y] + got[x, y]
    weight_part = (
        mine[0, 0]
        + over_visit(mine[1, 0], 1)
        + over_visit(mine[0, 1], 2)
        + over_visit(mine[1, 1], 3)
    )
    weight_sum = finish(weight_part)

    def run(x):
        first_row = ((my_x ^ x) * half).astype(jnp.int32)[None]
        return match(
            first_row, half, where, targets, quarters, table_rows, count, pixels, variances,
            table, col_band, row_band, depths,
        )

    keep_far, send_far = run(1)
    got_far = over_core(send_far)
    far = [keep_far[y] + got_far[y] for y in range(2)]
    from_x = over_visit(far[0], 1)
    from_xy = over_visit(far[1], 3)
    keep_near, send_near = run(0)
    got_near = over_core(send_near)
    near = [keep_near[y] + got_near[y] for y in range(2)]
    from_y = over_visit(near[1], 2)
    weighted_sum = finish(near[0] + from_x + from_y + from_xy)
    return weighted_sum[None], weight_sum[None]


def solution(mesh):
    placed = (
        P("visit", "patch", None, None, None),
        P("visit", "patch", None, None, None),
        P("visit", "patch", None),
        P("visit", "patch", None),
        P("visit", "patch", None),
        P("visit", "patch"),
        P(),
        P(),
        P(),
    )
    return jax.shard_map(
        on_device,
        mesh=mesh,
        in_specs=placed,
        out_specs=(P("patch", "visit", None), P("patch", "visit", None)),
        check_vma=False,
    )
```

```python
import functools

import jax
import jax.numpy as jnp
from jax import lax
from jax.experimental import pallas as pl
from jax.experimental.pallas import tpu as pltpu
from jax.sharding import PartitionSpec as P

f32 = jnp.float32
bf16 = jnp.bfloat16

SHARE = 1.0 / 32.0
KEEP = 1.0 - SHARE
VMEM_BYTES = 40 * 2**20
GROUP_ROWS = 256


def split_left(value):
    first = value.astype(bf16)
    return first, (value - KEEP * first.astype(f32)).astype(bf16)


def split_right(value):
    first = (KEEP * value).astype(bf16)
    return first, ((value - first.astype(f32)) * (1.0 / SHARE)).astype(bf16)


def relative(depth, own, depths):
    if depths & (depths - 1) == 0:
        return depth ^ own
    return lax.rem(depth - own + depths, depths)


def my_place(depths):
    patch_at = lax.axis_index("patch")
    visit_at = lax.axis_index("visit")
    return lax.rem(patch_at, 2), patch_at // 2, depths, visit_at // 2, lax.rem(visit_at, 2)


def place_of(where, target, quarter):
    core = lax.rem(target, 2) ^ where[0]
    depth = relative(target // 2, where[1], where[2])
    return core, depth, (quarter // 2) ^ where[3], lax.rem(quarter, 2)


def start_all(copies):
    for copy in copies:
        copy.start()


def wait_all(copies):
    for copy in copies:
        copy.wait()


def weight_kernel(
    targets_in, quarters_in, count_in, variance_in, keep_out, send_out,
    targets, quarters, count, variance, canvas, scalar_done, block_done, out_done,
):
    blocks, side, _ = variance.shape
    half = side // 2
    chunks = block_done.shape[0]
    size = blocks // chunks
    scalars = [
        pltpu.make_async_copy(a, b, scalar_done.at[i])
        for i, (a, b) in enumerate(
            [(targets_in, targets), (quarters_in, quarters), (count_in, count)]
        )
    ]
    arrays = [
        pltpu.make_async_copy(
            variance_in.at[pl.ds(i * size, size)],
            variance.at[pl.ds(i * size, size)],
            block_done.at[i],
        )
        for i in range(chunks)
    ]
    start_all(scalars)
    start_all(arrays)
    canvas[...] = jnp.zeros_like(canvas)
    where = my_place(canvas.shape[4])
    wait_all(scalars)

    def add_block(n, carry):
        live = jnp.where(n < count[0], 1.0, 0.0).astype(f32)
        inverse = live / variance[n]
        core, depth, down, across = place_of(where, targets[n], quarters[n])
        column = pl.ds(pl.multiple_of(across * side, side), side)
        for part in range(2):
            canvas[core, part ^ where[4], down, 0, depth, :, column] += inverse[
                part * half : (part + 1) * half
            ]
        return carry

    for i in range(chunks):
        arrays[i].wait()
        lax.fori_loop(i * size, (i + 1) * size, add_block, 0, unroll=2)
    outs = [
        pltpu.make_async_copy(canvas.at[1, :, :, 0], send_out, out_done.at[0]),
        pltpu.make_async_copy(canvas.at[0, :, :, 0], keep_out, out_done.at[1]),
    ]
    start_all(outs)
    wait_all(outs)


def sum_weights(targets, quarters, count, variance, depths):
    blocks, side, _ = variance.shape
    half = side // 2
    part = jax.ShapeDtypeStruct((2, 2, depths, half, 2 * side), f32)
    anywhere = pl.BlockSpec(memory_space=pltpu.HBM)
    return pl.pallas_call(
        weight_kernel,
        out_shape=(part, part),
        in_specs=[anywhere] * 4,
        out_specs=[anywhere] * 2,
        scratch_shapes=[
            pltpu.SMEM(targets.shape, jnp.int32),
            pltpu.SMEM(quarters.shape, jnp.int32),
            pltpu.SMEM(count.shape, jnp.int32),
            pltpu.VMEM(variance.shape, f32),
            pltpu.VMEM((2, 2, 2, 1, depths, half, 2 * side), f32),
            pltpu.SemaphoreType.DMA((3,)),
            pltpu.SemaphoreType.DMA((4,)),
            pltpu.SemaphoreType.DMA((2,)),
        ],
        compiler_params=pltpu.CompilerParams(vmem_limit_bytes=62 * 2**20),
        cost_estimate=pl.CostEstimate(flops=10**9, bytes_accessed=0, transcendentals=0),
    )(targets, quarters, count, variance)


def band_kernel(
    row_taps_in, col_taps_in, col_out, row_out, row_padded, col_padded, col_band, row_band, done
):
    nbasis, taps = row_taps_in.shape
    side = row_padded.shape[1]
    radius = (taps - 1) // 2
    row_padded[...] = jnp.zeros_like(row_padded)
    col_padded[...] = jnp.zeros_like(col_padded)
    row_padded[:, :taps] = row_taps_in[...]
    col_padded[:, :taps] = col_taps_in[...]
    row = lax.broadcasted_iota(jnp.int32, (side, side), 0)
    column = lax.broadcasted_iota(jnp.int32, (side, side), 1)
    near = jnp.abs(row - column) <= radius
    row_placed = pltpu.roll(row_padded[...], side - radius, 1)
    turn = (lax.rem(column - radius + row + side, side) == 0).astype(f32)
    col_placed = jnp.dot(
        col_padded[...], turn, precision=lax.Precision.HIGHEST, preferred_element_type=f32
    )
    for k in range(nbasis):
        base = jnp.broadcast_to(col_placed[k : k + 1], (side, side))
        band = jnp.where(near, pltpu.roll(base, 0, 1, stride=1, stride_axis=0), 0.0)
        first, second = split_left(band)
        col_band[k, :, :side] = first
        col_band[k, :, side:] = second
    col_copy = pltpu.make_async_copy(col_band, col_out, done.at[0])
    col_copy.start()
    for k in range(nbasis):
        base = jnp.broadcast_to(row_placed[k : k + 1], (side, side))
        band = jnp.where(near, pltpu.roll(base, 0, 1, stride=1, stride_axis=0), 0.0)
        first, second = split_right(band)
        row_band[k, :side, :] = first
        row_band[k, side:, :] = second
    row_copy = pltpu.make_async_copy(row_band, row_out, done.at[1])
    row_copy.start()
    col_copy.wait()
    row_copy.wait()


def make_bands(row_taps, col_taps, side):
    nbasis, taps = row_taps.shape
    anywhere = pl.BlockSpec(memory_space=pltpu.HBM)
    col_shape, row_shape = (nbasis, side, 2 * side), (nbasis, 2 * side, side)
    tap_block = pl.BlockSpec((nbasis, taps), lambda i: (0, 0))
    return pl.pallas_call(
        band_kernel,
        grid=(1,),
        out_shape=(
            jax.ShapeDtypeStruct(col_shape, bf16),
            jax.ShapeDtypeStruct(row_shape, bf16),
        ),
        in_specs=[tap_block] * 2,
        out_specs=[anywhere] * 2,
        scratch_shapes=[
            pltpu.VMEM((nbasis, side), f32),
            pltpu.VMEM((nbasis, side), f32),
            pltpu.VMEM(col_shape, bf16),
            pltpu.VMEM(row_shape, bf16),
            pltpu.SemaphoreType.DMA((2,)),
        ],
        compiler_params=pltpu.CompilerParams(vmem_limit_bytes=VMEM_BYTES),
        cost_estimate=pl.CostEstimate(flops=10**9, bytes_accessed=0, transcendentals=0),
    )(row_taps, col_taps)


def match_kernel(
    offset, targets_in, quarters_in, rows_in, count_in, pixels_in, variance_in, table_in,
    col_in, row_in, keep_out, send_out,
    targets, quarters, table_rows, count, pixels, variance, table, col_band, row_band, canvas,
    total, coefficients, scalar_done, array_done, pixel_done, variance_done, out_done,
):
    blocks, side, _ = pixels.shape
    nbasis, rows, _ = col_band.shape
    group = total.shape[0]
    far, start = offset
    where = my_place(canvas.shape[2])
    top = pl.multiple_of((where[4] ^ far) * (side // 2) + start, rows)
    scalars = [
        pltpu.make_async_copy(a, b, scalar_done.at[i])
        for i, (a, b) in enumerate(
            [(targets_in, targets), (quarters_in, quarters), (rows_in, table_rows),
             (count_in, count)]
        )
    ]
    copy_col = pltpu.make_async_copy(col_in.at[:, pl.ds(top, rows)], col_band, array_done.at[0])
    copy_row = pltpu.make_async_copy(row_in, row_band, array_done.at[1])
    copy_table = pltpu.make_async_copy(table_in, table, array_done.at[2])

    def pixel_copy(j):
        at = pl.ds(j * group, group)
        return pltpu.make_async_copy(pixels_in.at[at], pixels.at[at], pixel_done.at[j])

    def variance_copy(j):
        at = pl.ds(j * group, group)
        return pltpu.make_async_copy(
            variance_in.at[at, pl.ds(top, rows)], variance.at[at], variance_done.at[j]
        )

    start_all(scalars)
    copy_table.start()
    copy_col.start()
    pixel_copy(0).start()
    copy_row.start()
    variance_copy(0).start()
    for j in range(1, blocks // group):
        pixel_copy(j).start()
        variance_copy(j).start()
    canvas[...] = jnp.zeros_like(canvas)
    entries = table.shape[2]
    copy_table.wait()
    coefficients[:, :, :entries] = table[...]
    lane = lax.broadcasted_iota(jnp.int32, (1, side), 1).astype(f32)
    sub = lax.broadcasted_iota(jnp.int32, (8, side), 0).astype(f32)
    step = 8.0 / side
    wait_all(scalars)
    copy_col.wait()
    copy_row.wait()

    def add_group(j, carry):
        pixel_copy(j).wait()
        variance_copy(j).wait()
        terms = []
        for member in range(group):
            n = group * j + member
            quarter = quarters[n]
            across = (lane + 0.5) / side - 1.0 + lax.rem(quarter, 2).astype(f32)
            down = (sub + 0.5 + top.astype(f32)) / side - 1.0 + (quarter // 2).astype(f32)
            entry = table_rows[n]
            chunk = coefficients[:, :, pl.ds(pl.multiple_of((entry // 128) * 128, 128), 128)]
            chunk = chunk.reshape(-1, 128)
            chunk = pltpu.roll(chunk, lax.rem(128 - lax.rem(entry, 128), 128), 1)
            poly = jnp.broadcast_to(chunk[:, :1], (chunk.shape[0], side))
            poly = [poly[i * nbasis : (i + 1) * nbasis] for i in range(chunk.shape[0] // nbasis)]
            constant = poly[0] + across * (poly[1] + across * poly[3])
            linear = poly[2] + across * poly[4]
            terms.append((constant, linear, poly[5], down))
        left = col_band[...].reshape(nbasis * rows, 2 * side)
        halves = []
        for pair in range(group // 2):
            n = group * j + 2 * pair
            both = jnp.concatenate([pixels[n], pixels[n + 1]], axis=1)
            right = jnp.concatenate(split_right(both), axis=0)
            convolved = jnp.dot(left, right, preferred_element_type=f32)
            halves.append(split_left(convolved))
        for k in range(nbasis):
            at = slice(k * rows, (k + 1) * rows)
            stacked = []
            for member in range(group):
                first, second = halves[member // 2]
                lanes = slice((member % 2) * side, (member % 2 + 1) * side)
                stacked.append(jnp.concatenate([first[at, lanes], second[at, lanes]], axis=1))
            spread = jnp.dot(
                jnp.concatenate(stacked, axis=0), row_band[k], preferred_element_type=f32
            )
            for member in range(group):
                constant, linear, square, down = terms[member]
                b, d = linear[k : k + 1], square[k : k + 1]
                weight = constant[k : k + 1] + down * (b + down * d)
                change = step * b + d * (2.0 * step * down + step * step)
                second_change = (2.0 * step * step) * d
                for i in range(rows // 8):
                    value = weight * spread[member * rows + 8 * i : member * rows + 8 * i + 8]
                    if k == 0:
                        total[member, 8 * i : 8 * i + 8] = value
                    else:
                        total[member, 8 * i : 8 * i + 8] += value
                    if i < rows // 8 - 1:
                        weight = weight + change
                        change = change + second_change
        for member in range(group):
            n = group * j + member
            live = jnp.where(n < count[0], 1.0, 0.0).astype(f32)
            core, depth, down, across = place_of(where, targets[n], quarters[n])
            column = pl.ds(pl.multiple_of(across * side, side), side)
            canvas[core, down, depth, :, column] += (live / variance[n]) * total[member]
        return carry

    lax.fori_loop(0, blocks // group, add_group, 0)
    outs = [
        pltpu.make_async_copy(canvas.at[1], send_out, out_done.at[0]),
        pltpu.make_async_copy(canvas.at[0], keep_out, out_done.at[1]),
    ]
    start_all(outs)
    wait_all(outs)


def match(
    offset, rows, targets, quarters, table_rows, count, pixels, variance, table,
    col_band, row_band, depths,
):
    blocks, side, _ = pixels.shape
    nbasis = col_band.shape[0]
    group = min(blocks, GROUP_ROWS // rows)
    part = jax.ShapeDtypeStruct((2, depths, rows, 2 * side), f32)
    anywhere = pl.BlockSpec(memory_space=pltpu.HBM)
    entries = -(-table.shape[2] // 128) * 128
    scalars = (targets, quarters, table_rows, count)
    return pl.pallas_call(
        functools.partial(match_kernel, offset),
        out_shape=(part, part),
        in_specs=[anywhere] * 9,
        out_specs=[anywhere] * 2,
        scratch_shapes=[pltpu.SMEM(a.shape, jnp.int32) for a in scalars]
        + [
            pltpu.VMEM(pixels.shape, f32),
            pltpu.VMEM((blocks, rows, side), f32),
            pltpu.VMEM(table.shape, f32),
            pltpu.VMEM((nbasis, rows, 2 * side), bf16),
            pltpu.VMEM(row_band.shape, bf16),
            pltpu.VMEM((2, 2, depths, rows, 2 * side), f32),
            pltpu.VMEM((group, rows, side), f32),
            pltpu.VMEM(table.shape[:2] + (entries,), f32),
            pltpu.SemaphoreType.DMA((4,)),
            pltpu.SemaphoreType.DMA((3,)),
            pltpu.SemaphoreType.DMA((blocks // group,)),
            pltpu.SemaphoreType.DMA((blocks // group,)),
            pltpu.SemaphoreType.DMA((2,)),
        ],
        compiler_params=pltpu.CompilerParams(vmem_limit_bytes=VMEM_BYTES),
        cost_estimate=pl.CostEstimate(
            flops=blocks * rows * side * 40960, bytes_accessed=10**7, transcendentals=0
        ),
    )(*scalars, pixels, variance, table, col_band, row_band)


def on_device(
    image, variance, dest_patch, quadrant, coef_index, block_count, coef_table, row_taps, col_taps
):
    pixels = image[0, 0]
    variances = variance[0, 0]
    targets = dest_patch[0, 0]
    quarters = quadrant[0, 0]
    table_rows = coef_index[0, 0]
    count = block_count[0]
    owners = lax.axis_size("patch")
    visits = lax.axis_size("visit")
    depths = owners // 2
    side = pixels.shape[1]
    half = side // 2
    table = jnp.transpose(coef_table, (2, 1, 0))
    together = lax.optimization_barrier

    def over_core(value):
        return lax.ppermute(value, "patch", [(i, i ^ 1) for i in range(owners)])

    def over_visit(value, flip):
        return lax.ppermute(value, "visit", [(i, i ^ flip) for i in range(visits)])

    def over_depth(value, shift):
        if depths & (depths - 1) == 0:
            pairs = [(i, i ^ (2 * shift)) for i in range(owners)]
        else:
            pairs = [(i, (i + 2 * shift) % owners) for i in range(owners)]
        return lax.ppermute(value, "patch", pairs)

    def pieces_of(value):
        return [over_depth(value[s], s) for s in range(1, depths)]

    def run(offset, rows, bands):
        return match(
            offset, rows, targets, quarters, table_rows, count, pixels, variances,
            table, bands[0], bands[1], depths,
        )

    keep, send = sum_weights(targets, quarters, count, variances, depths)
    got = over_core(send)
    row_taps, col_taps, keep = together((row_taps, col_taps, keep))
    bands = make_bands(row_taps, col_taps, side)
    got, bands = together((got, bands))
    weight_far, weight_near = keep[1] + got[1], keep[0] + got[0]
    weight_far, weight_near, bands = together((weight_far, weight_near, bands))
    weight_x = over_visit(weight_far, 1)
    keep_far, send_far = run((1, 0), half, bands)
    keep_far, send_far, weight_x = together((keep_far, send_far, weight_x))
    got_far = over_core(send_far)
    weight_near, weight_next = weight_near[0] + weight_x[0], weight_near[1] + weight_x[1]
    weight_near, weight_next, got_far = together((weight_near, weight_next, got_far))
    weight_y = over_visit(weight_next, 2)
    far = keep_far + got_far
    far, bands = together((far, bands))
    far_x = over_visit(far, 1)
    keep_near, send_near = run((0, 0), half, bands)
    keep_near, send_near, weight_y, far_x = together((keep_near, send_near, weight_y, far_x))
    got_near = over_core(send_near)
    weight_part = weight_near + weight_y
    weight_part, got_near = together((weight_part, got_near))
    near = [keep_near[y] + got_near[y] + far_x[y] for y in range(2)]
    near_y = over_visit(near[1], 2)
    weight_part, near = together((weight_part, near))
    weight_pieces = pieces_of(weight_part)
    part = near[0] + near_y
    weighted_sum = functools.reduce(jnp.add, pieces_of(part), part[0])
    weight_sum = functools.reduce(jnp.add, weight_pieces, weight_part[0])
    return weighted_sum[None], weight_sum[None]


def solution(mesh):
    placed = (
        P("visit", "patch", None, None, None),
        P("visit", "patch", None, None, None),
        P("visit", "patch", None),
        P("visit", "patch", None),
        P("visit", "patch", None),
        P("visit", "patch"),
        P(),
        P(),
        P(),
    )
    return jax.shard_map(
        on_device,
        mesh=mesh,
        in_specs=placed,
        out_specs=(P("patch", "visit", None), P("patch", "visit", None)),
        check_vma=False,
    )
```

```python
import functools

import jax
import jax.numpy as jnp
from jax import lax
from jax.experimental import pallas as pl
from jax.experimental.pallas import tpu as pltpu
from jax.sharding import PartitionSpec as P

f32 = jnp.float32
bf16 = jnp.bfloat16

SHARE = 1.0 / 32.0
KEEP = 1.0 - SHARE
VMEM_BYTES = 40 * 2**20
GROUP_ROWS = 512


def split_left(value):
    first = value.astype(bf16)
    return first, (value - KEEP * first.astype(f32)).astype(bf16)


def split_right(value):
    first = (KEEP * value).astype(bf16)
    return first, ((value - first.astype(f32)) * (1.0 / SHARE)).astype(bf16)


def relative(depth, own, depths):
    if depths & (depths - 1) == 0:
        return depth ^ own
    return lax.rem(depth - own + depths, depths)


def my_place(depths):
    patch_at = lax.axis_index("patch")
    visit_at = lax.axis_index("visit")
    return lax.rem(patch_at, 2), patch_at // 2, depths, visit_at // 2, lax.rem(visit_at, 2)


def place_of(where, target, quarter):
    core = lax.rem(target, 2) ^ where[0]
    depth = relative(target // 2, where[1], where[2])
    return core, depth, (quarter // 2) ^ where[3], lax.rem(quarter, 2)


def start_all(copies):
    for copy in copies:
        copy.start()


def wait_all(copies):
    for copy in copies:
        copy.wait()


def weight_kernel(
    targets_in, quarters_in, count_in, variance_in, keep_out, send_out,
    targets, quarters, count, variance, canvas, scalar_done, block_done, out_done,
):
    blocks, side, _ = variance.shape
    half = side // 2
    chunks = block_done.shape[0]
    size = blocks // chunks
    scalars = [
        pltpu.make_async_copy(a, b, scalar_done.at[i])
        for i, (a, b) in enumerate(
            [(targets_in, targets), (quarters_in, quarters), (count_in, count)]
        )
    ]
    arrays = [
        pltpu.make_async_copy(
            variance_in.at[pl.ds(i * size, size)],
            variance.at[pl.ds(i * size, size)],
            block_done.at[i],
        )
        for i in range(chunks)
    ]
    start_all(scalars)
    start_all(arrays)
    canvas[...] = jnp.zeros_like(canvas)
    where = my_place(canvas.shape[4])
    wait_all(scalars)

    def add_block(n, carry):
        live = jnp.where(n < count[0], 1.0, 0.0).astype(f32)
        inverse = live / variance[n]
        core, depth, down, across = place_of(where, targets[n], quarters[n])
        column = pl.ds(pl.multiple_of(across * side, side), side)
        for part in range(2):
            canvas[core, part ^ where[4], down, 0, depth, :, column] += inverse[
                part * half : (part + 1) * half
            ]
        return carry

    for i in range(chunks):
        arrays[i].wait()
        lax.fori_loop(i * size, (i + 1) * size, add_block, 0, unroll=2)
    outs = [
        pltpu.make_async_copy(canvas.at[1, :, :, 0], send_out, out_done.at[0]),
        pltpu.make_async_copy(canvas.at[0, :, :, 0], keep_out, out_done.at[1]),
    ]
    start_all(outs)
    wait_all(outs)


def sum_weights(targets, quarters, count, variance, depths):
    blocks, side, _ = variance.shape
    half = side // 2
    part = jax.ShapeDtypeStruct((2, 2, depths, half, 2 * side), f32)
    anywhere = pl.BlockSpec(memory_space=pltpu.HBM)
    return pl.pallas_call(
        weight_kernel,
        out_shape=(part, part),
        in_specs=[anywhere] * 4,
        out_specs=[anywhere] * 2,
        scratch_shapes=[
            pltpu.SMEM(targets.shape, jnp.int32),
            pltpu.SMEM(quarters.shape, jnp.int32),
            pltpu.SMEM(count.shape, jnp.int32),
            pltpu.VMEM(variance.shape, f32),
            pltpu.VMEM((2, 2, 2, 1, depths, half, 2 * side), f32),
            pltpu.SemaphoreType.DMA((3,)),
            pltpu.SemaphoreType.DMA((4,)),
            pltpu.SemaphoreType.DMA((2,)),
        ],
        compiler_params=pltpu.CompilerParams(vmem_limit_bytes=62 * 2**20),
        cost_estimate=pl.CostEstimate(flops=10**9, bytes_accessed=0, transcendentals=0),
    )(targets, quarters, count, variance)


def band_kernel(
    row_taps_in, col_taps_in, col_out, row_out, row_padded, col_padded, col_band, row_band, done
):
    nbasis, taps = row_taps_in.shape
    side = row_padded.shape[1]
    radius = (taps - 1) // 2
    row_padded[...] = jnp.zeros_like(row_padded)
    col_padded[...] = jnp.zeros_like(col_padded)
    row_padded[:, :taps] = row_taps_in[...]
    col_padded[:, :taps] = col_taps_in[...]
    row = lax.broadcasted_iota(jnp.int32, (side, side), 0)
    column = lax.broadcasted_iota(jnp.int32, (side, side), 1)
    near = jnp.abs(row - column) <= radius
    row_placed = pltpu.roll(row_padded[...], side - radius, 1)
    turn = (lax.rem(column - radius + row + side, side) == 0).astype(f32)
    col_placed = jnp.dot(
        col_padded[...], turn, precision=lax.Precision.HIGHEST, preferred_element_type=f32
    )
    for k in range(nbasis):
        base = jnp.broadcast_to(col_placed[k : k + 1], (side, side))
        band = jnp.where(near, pltpu.roll(base, 0, 1, stride=1, stride_axis=0), 0.0)
        first, second = split_left(band)
        col_band[k, :, :side] = first
        col_band[k, :, side:] = second
    col_copy = pltpu.make_async_copy(col_band, col_out, done.at[0])
    col_copy.start()
    for k in range(nbasis):
        base = jnp.broadcast_to(row_placed[k : k + 1], (side, side))
        band = jnp.where(near, pltpu.roll(base, 0, 1, stride=1, stride_axis=0), 0.0)
        first, second = split_right(band)
        row_band[k, :side, :] = first
        row_band[k, side:, :] = second
    row_copy = pltpu.make_async_copy(row_band, row_out, done.at[1])
    row_copy.start()
    col_copy.wait()
    row_copy.wait()


def make_bands(row_taps, col_taps, side):
    nbasis, taps = row_taps.shape
    anywhere = pl.BlockSpec(memory_space=pltpu.HBM)
    col_shape, row_shape = (nbasis, side, 2 * side), (nbasis, 2 * side, side)
    tap_block = pl.BlockSpec((nbasis, taps), lambda i: (0, 0))
    return pl.pallas_call(
        band_kernel,
        grid=(1,),
        out_shape=(
            jax.ShapeDtypeStruct(col_shape, bf16),
            jax.ShapeDtypeStruct(row_shape, bf16),
        ),
        in_specs=[tap_block] * 2,
        out_specs=[anywhere] * 2,
        scratch_shapes=[
            pltpu.VMEM((nbasis, side), f32),
            pltpu.VMEM((nbasis, side), f32),
            pltpu.VMEM(col_shape, bf16),
            pltpu.VMEM(row_shape, bf16),
            pltpu.SemaphoreType.DMA((2,)),
        ],
        compiler_params=pltpu.CompilerParams(vmem_limit_bytes=VMEM_BYTES),
        cost_estimate=pl.CostEstimate(flops=10**9, bytes_accessed=0, transcendentals=0),
    )(row_taps, col_taps)


def match_kernel(
    offset, targets_in, quarters_in, rows_in, count_in, pixels_in, variance_in, table_in,
    col_in, row_in, keep_out, send_out,
    targets, quarters, table_rows, count, pixels, variance, table, col_band, row_band, canvas,
    total, coefficients, scalar_done, array_done, pixel_done, variance_done, out_done,
):
    blocks, side, _ = pixels.shape
    nbasis, rows, _ = col_band.shape
    group = total.shape[0]
    far, start = offset
    where = my_place(canvas.shape[2])
    top = pl.multiple_of((where[4] ^ far) * (side // 2) + start, rows)
    scalars = [
        pltpu.make_async_copy(a, b, scalar_done.at[i])
        for i, (a, b) in enumerate(
            [(targets_in, targets), (quarters_in, quarters), (rows_in, table_rows),
             (count_in, count)]
        )
    ]
    copy_col = pltpu.make_async_copy(col_in.at[:, pl.ds(top, rows)], col_band, array_done.at[0])
    copy_row = pltpu.make_async_copy(row_in, row_band, array_done.at[1])
    copy_table = pltpu.make_async_copy(table_in, table, array_done.at[2])

    def pixel_copy(j):
        at = pl.ds(j * group, group)
        return pltpu.make_async_copy(pixels_in.at[at], pixels.at[at], pixel_done.at[j])

    def variance_copy(j):
        at = pl.ds(j * group, group)
        return pltpu.make_async_copy(
            variance_in.at[at, pl.ds(top, rows)], variance.at[at], variance_done.at[j]
        )

    start_all(scalars)
    copy_table.start()
    copy_col.start()
    pixel_copy(0).start()
    copy_row.start()
    variance_copy(0).start()
    for j in range(1, blocks // group):
        pixel_copy(j).start()
        variance_copy(j).start()
    canvas[...] = jnp.zeros_like(canvas)
    entries = table.shape[2]
    copy_table.wait()
    coefficients[:, :, :entries] = table[...]
    lane = lax.broadcasted_iota(jnp.int32, (1, side), 1).astype(f32)
    sub = lax.broadcasted_iota(jnp.int32, (8, side), 0).astype(f32)
    step = 8.0 / side
    wait_all(scalars)
    copy_col.wait()
    copy_row.wait()

    def add_group(j, carry):
        pixel_copy(j).wait()
        variance_copy(j).wait()
        terms = []
        for member in range(group):
            n = group * j + member
            quarter = quarters[n]
            across = (lane + 0.5) / side - 1.0 + lax.rem(quarter, 2).astype(f32)
            down = (sub + 0.5 + top.astype(f32)) / side - 1.0 + (quarter // 2).astype(f32)
            entry = table_rows[n]
            chunk = coefficients[:, :, pl.ds(pl.multiple_of((entry // 128) * 128, 128), 128)]
            chunk = chunk.reshape(-1, 128)
            chunk = pltpu.roll(chunk, lax.rem(128 - lax.rem(entry, 128), 128), 1)
            poly = jnp.broadcast_to(chunk[:, :1], (chunk.shape[0], side))
            poly = [poly[i * nbasis : (i + 1) * nbasis] for i in range(chunk.shape[0] // nbasis)]
            constant = poly[0] + across * (poly[1] + across * poly[3])
            linear = poly[2] + across * poly[4]
            terms.append((constant, linear, poly[5], down))
        left = col_band[...].reshape(nbasis * rows, 2 * side)
        halves = []
        for pair in range(group // 2):
            n = group * j + 2 * pair
            both = jnp.concatenate([pixels[n], pixels[n + 1]], axis=1)
            right = jnp.concatenate(split_right(both), axis=0)
            convolved = jnp.dot(left, right, preferred_element_type=f32)
            halves.append(split_left(convolved))
        for k in range(nbasis):
            at = slice(k * rows, (k + 1) * rows)
            stacked = []
            for member in range(group):
                first, second = halves[member // 2]
                lanes = slice((member % 2) * side, (member % 2 + 1) * side)
                stacked.append(jnp.concatenate([first[at, lanes], second[at, lanes]], axis=1))
            spread = jnp.dot(
                jnp.concatenate(stacked, axis=0), row_band[k], preferred_element_type=f32
            )
            for member in range(group):
                constant, linear, square, down = terms[member]
                b, d = linear[k : k + 1], square[k : k + 1]
                weight = constant[k : k + 1] + down * (b + down * d)
                change = step * b + d * (2.0 * step * down + step * step)
                second_change = (2.0 * step * step) * d
                for i in range(rows // 8):
                    value = weight * spread[member * rows + 8 * i : member * rows + 8 * i + 8]
                    if k == 0:
                        total[member, 8 * i : 8 * i + 8] = value
                    else:
                        total[member, 8 * i : 8 * i + 8] += value
                    if i < rows // 8 - 1:
                        weight = weight + change
                        change = change + second_change
        for member in range(group):
            n = group * j + member
            live = jnp.where(n < count[0], 1.0, 0.0).astype(f32)
            core, depth, down, across = place_of(where, targets[n], quarters[n])
            column = pl.ds(pl.multiple_of(across * side, side), side)
            canvas[core, down, depth, :, column] += (live / variance[n]) * total[member]
        return carry

    lax.fori_loop(0, blocks // group, add_group, 0)
    outs = [
        pltpu.make_async_copy(canvas.at[1], send_out, out_done.at[0]),
        pltpu.make_async_copy(canvas.at[0], keep_out, out_done.at[1]),
    ]
    start_all(outs)
    wait_all(outs)


def match(
    offset, rows, targets, quarters, table_rows, count, pixels, variance, table,
    col_band, row_band, depths,
):
    blocks, side, _ = pixels.shape
    nbasis = col_band.shape[0]
    group = min(blocks, GROUP_ROWS // rows)
    part = jax.ShapeDtypeStruct((2, depths, rows, 2 * side), f32)
    anywhere = pl.BlockSpec(memory_space=pltpu.HBM)
    entries = -(-table.shape[2] // 128) * 128
    scalars = (targets, quarters, table_rows, count)
    return pl.pallas_call(
        functools.partial(match_kernel, offset),
        out_shape=(part, part),
        in_specs=[anywhere] * 9,
        out_specs=[anywhere] * 2,
        scratch_shapes=[pltpu.SMEM(a.shape, jnp.int32) for a in scalars]
        + [
            pltpu.VMEM(pixels.shape, f32),
            pltpu.VMEM((blocks, rows, side), f32),
            pltpu.VMEM(table.shape, f32),
            pltpu.VMEM((nbasis, rows, 2 * side), bf16),
            pltpu.VMEM(row_band.shape, bf16),
            pltpu.VMEM((2, 2, depths, rows, 2 * side), f32),
            pltpu.VMEM((group, rows, side), f32),
            pltpu.VMEM(table.shape[:2] + (entries,), f32),
            pltpu.SemaphoreType.DMA((4,)),
            pltpu.SemaphoreType.DMA((3,)),
            pltpu.SemaphoreType.DMA((blocks // group,)),
            pltpu.SemaphoreType.DMA((blocks // group,)),
            pltpu.SemaphoreType.DMA((2,)),
        ],
        compiler_params=pltpu.CompilerParams(vmem_limit_bytes=VMEM_BYTES),
        cost_estimate=pl.CostEstimate(
            flops=blocks * rows * side * 40960, bytes_accessed=10**7, transcendentals=0
        ),
    )(*scalars, pixels, variance, table, col_band, row_band)


def on_device(
    image, variance, dest_patch, quadrant, coef_index, block_count, coef_table, row_taps, col_taps
):
    pixels = image[0, 0]
    variances = variance[0, 0]
    targets = dest_patch[0, 0]
    quarters = quadrant[0, 0]
    table_rows = coef_index[0, 0]
    count = block_count[0]
    owners = lax.axis_size("patch")
    visits = lax.axis_size("visit")
    depths = owners // 2
    side = pixels.shape[1]
    half = side // 2
    table = jnp.transpose(coef_table, (2, 1, 0))
    together = lax.optimization_barrier

    def over_core(value):
        return lax.ppermute(value, "patch", [(i, i ^ 1) for i in range(owners)])

    def over_visit(value, flip):
        return lax.ppermute(value, "visit", [(i, i ^ flip) for i in range(visits)])

    def over_depth(value, shift):
        if depths & (depths - 1) == 0:
            pairs = [(i, i ^ (2 * shift)) for i in range(owners)]
        else:
            pairs = [(i, (i + 2 * shift) % owners) for i in range(owners)]
        return lax.ppermute(value, "patch", pairs)

    def pieces_of(value):
        return [over_depth(value[s], s) for s in range(1, depths)]

    def run(offset, rows, bands):
        return match(
            offset, rows, targets, quarters, table_rows, count, pixels, variances,
            table, bands[0], bands[1], depths,
        )

    keep, send = sum_weights(targets, quarters, count, variances, depths)
    got = over_core(send)
    row_taps, col_taps, keep = together((row_taps, col_taps, keep))
    bands = make_bands(row_taps, col_taps, side)
    got, bands = together((got, bands))
    weight_far, weight_near = keep[1] + got[1], keep[0] + got[0]
    weight_far, weight_near, bands = together((weight_far, weight_near, bands))
    weight_x = over_visit(weight_far, 1)
    keep_far, send_far = run((1, 0), half, bands)
    got_far = over_core(send_far)
    keep_far, weight_x = together((keep_far, weight_x))
    weight_near, weight_next = weight_near[0] + weight_x[0], weight_near[1] + weight_x[1]
    weight_near, weight_next, got_far = together((weight_near, weight_next, got_far))
    far = keep_far + got_far
    far, weight_next, bands = together((far, weight_next, bands))
    weight_y = over_visit(weight_next, 2)
    far_x = over_visit(far, 1)
    keep_near, send_near = run((0, 0), half, bands)
    send_near, weight_y = together((send_near, weight_y))
    got_near = over_core(send_near)
    weight_part = weight_near + weight_y
    keep_near, weight_part, far_x = together((keep_near, weight_part, far_x))
    weight_pieces = pieces_of(weight_part)
    near = [keep_near[y] + far_x[y] for y in range(2)]
    near, got_near = together((near, got_near))
    near = [near[y] + got_near[y] for y in range(2)]
    near_y = over_visit(near[1], 2)
    part = near[0] + near_y
    pieces = pieces_of(part)
    weight_part, part = together((weight_part, part))
    weight_sum = functools.reduce(jnp.add, weight_pieces, weight_part[0])
    weighted_sum = functools.reduce(jnp.add, pieces, part[0])
    return weighted_sum[None], weight_sum[None]


def solution(mesh):
    placed = (
        P("visit", "patch", None, None, None),
        P("visit", "patch", None, None, None),
        P("visit", "patch", None),
        P("visit", "patch", None),
        P("visit", "patch", None),
        P("visit", "patch"),
        P(),
        P(),
        P(),
    )
    return jax.shard_map(
        on_device,
        mesh=mesh,
        in_specs=placed,
        out_specs=(P("patch", "visit", None), P("patch", "visit", None)),
        check_vma=False,
    )
```

```python
import functools

import jax
import jax.numpy as jnp
from jax import lax
from jax.experimental import pallas as pl
from jax.experimental.pallas import tpu as pltpu
from jax.sharding import PartitionSpec as P

f32 = jnp.float32
bf16 = jnp.bfloat16

SHARE = 1.0 / 32.0
KEEP = 1.0 - SHARE
VMEM_BYTES = 40 * 2**20
GROUP_ROWS = 512


def split_left(value):
    first = value.astype(bf16)
    return first, (value - KEEP * first.astype(f32)).astype(bf16)


def split_right(value):
    first = (KEEP * value).astype(bf16)
    return first, ((value - first.astype(f32)) * (1.0 / SHARE)).astype(bf16)


def relative(depth, own, depths):
    if depths & (depths - 1) == 0:
        return depth ^ own
    return lax.rem(depth - own + depths, depths)


def my_place(depths):
    patch_at = lax.axis_index("patch")
    visit_at = lax.axis_index("visit")
    return lax.rem(patch_at, 2), patch_at // 2, depths, visit_at // 2, lax.rem(visit_at, 2)


def place_of(where, target, quarter):
    core = lax.rem(target, 2) ^ where[0]
    depth = relative(target // 2, where[1], where[2])
    return core, depth, (quarter // 2) ^ where[3], lax.rem(quarter, 2)


def start_all(copies):
    for copy in copies:
        copy.start()


def wait_all(copies):
    for copy in copies:
        copy.wait()


def weight_kernel(
    targets_in, quarters_in, count_in, variance_in, keep_out, send_out,
    targets, quarters, count, variance, canvas, scalar_done, block_done, out_done,
):
    blocks, side, _ = variance.shape
    half = side // 2
    chunks = block_done.shape[0]
    size = blocks // chunks
    scalars = [
        pltpu.make_async_copy(a, b, scalar_done.at[i])
        for i, (a, b) in enumerate(
            [(targets_in, targets), (quarters_in, quarters), (count_in, count)]
        )
    ]
    arrays = [
        pltpu.make_async_copy(
            variance_in.at[pl.ds(i * size, size)],
            variance.at[pl.ds(i * size, size)],
            block_done.at[i],
        )
        for i in range(chunks)
    ]
    start_all(scalars)
    start_all(arrays)
    canvas[...] = jnp.zeros_like(canvas)
    where = my_place(2 * canvas.shape[4])
    wait_all(scalars)

    def add_block(n, carry):
        live = jnp.where(n < count[0], 1.0, 0.0).astype(f32)
        inverse = live / variance[n]
        core, depth, down, across = place_of(where, targets[n], quarters[n])
        column = pl.ds(pl.multiple_of(across * side, side), side)
        for part in range(2):
            canvas[
                core, lax.rem(depth, 2), part ^ where[4], down, depth // 2, :, column
            ] += inverse[
                part * half : (part + 1) * half
            ]
        return carry

    for i in range(chunks):
        arrays[i].wait()
        lax.fori_loop(i * size, (i + 1) * size, add_block, 0, unroll=2)
    outs = [
        pltpu.make_async_copy(canvas.at[1], send_out, out_done.at[0]),
        pltpu.make_async_copy(canvas.at[0], keep_out, out_done.at[1]),
    ]
    start_all(outs)
    wait_all(outs)


def sum_weights(targets, quarters, count, variance, depths):
    blocks, side, _ = variance.shape
    half = side // 2
    part = jax.ShapeDtypeStruct((2, 2, 2, depths // 2, half, 2 * side), f32)
    anywhere = pl.BlockSpec(memory_space=pltpu.HBM)
    return pl.pallas_call(
        weight_kernel,
        out_shape=(part, part),
        in_specs=[anywhere] * 4,
        out_specs=[anywhere] * 2,
        scratch_shapes=[
            pltpu.SMEM(targets.shape, jnp.int32),
            pltpu.SMEM(quarters.shape, jnp.int32),
            pltpu.SMEM(count.shape, jnp.int32),
            pltpu.VMEM(variance.shape, f32),
            pltpu.VMEM((2,) + part.shape, f32),
            pltpu.SemaphoreType.DMA((3,)),
            pltpu.SemaphoreType.DMA((4,)),
            pltpu.SemaphoreType.DMA((2,)),
        ],
        compiler_params=pltpu.CompilerParams(vmem_limit_bytes=VMEM_BYTES),
        cost_estimate=pl.CostEstimate(flops=10**9, bytes_accessed=0, transcendentals=0),
    )(targets, quarters, count, variance)


def band_kernel(
    row_taps_in, col_taps_in, col_out, row_out, row_padded, col_padded, col_band, row_band, done
):
    nbasis, taps = row_taps_in.shape
    side = row_padded.shape[1]
    radius = (taps - 1) // 2
    row_padded[...] = jnp.zeros_like(row_padded)
    col_padded[...] = jnp.zeros_like(col_padded)
    row_padded[:, :taps] = row_taps_in[...]
    col_padded[:, :taps] = col_taps_in[...]
    row = lax.broadcasted_iota(jnp.int32, (side, side), 0)
    column = lax.broadcasted_iota(jnp.int32, (side, side), 1)
    near = jnp.abs(row - column) <= radius
    row_placed = pltpu.roll(row_padded[...], side - radius, 1)
    turn = (lax.rem(column - radius + row + side, side) == 0).astype(f32)
    col_placed = jnp.dot(
        col_padded[...], turn, precision=lax.Precision.HIGHEST, preferred_element_type=f32
    )
    for k in range(nbasis):
        base = jnp.broadcast_to(col_placed[k : k + 1], (side, side))
        band = jnp.where(near, pltpu.roll(base, 0, 1, stride=1, stride_axis=0), 0.0)
        first, second = split_left(band)
        col_band[k, :, :side] = first
        col_band[k, :, side:] = second
    col_copy = pltpu.make_async_copy(col_band, col_out, done.at[0])
    col_copy.start()
    for k in range(nbasis):
        base = jnp.broadcast_to(row_placed[k : k + 1], (side, side))
        band = jnp.where(near, pltpu.roll(base, 0, 1, stride=1, stride_axis=0), 0.0)
        first, second = split_right(band)
        row_band[k, :side, :] = first
        row_band[k, side:, :] = second
    row_copy = pltpu.make_async_copy(row_band, row_out, done.at[1])
    row_copy.start()
    col_copy.wait()
    row_copy.wait()


def make_bands(row_taps, col_taps, side):
    nbasis, taps = row_taps.shape
    anywhere = pl.BlockSpec(memory_space=pltpu.HBM)
    col_shape, row_shape = (nbasis, side, 2 * side), (nbasis, 2 * side, side)
    tap_block = pl.BlockSpec((nbasis, taps), lambda i: (0, 0))
    return pl.pallas_call(
        band_kernel,
        grid=(1,),
        out_shape=(
            jax.ShapeDtypeStruct(col_shape, bf16),
            jax.ShapeDtypeStruct(row_shape, bf16),
        ),
        in_specs=[tap_block] * 2,
        out_specs=[anywhere] * 2,
        scratch_shapes=[
            pltpu.VMEM((nbasis, side), f32),
            pltpu.VMEM((nbasis, side), f32),
            pltpu.VMEM(col_shape, bf16),
            pltpu.VMEM(row_shape, bf16),
            pltpu.SemaphoreType.DMA((2,)),
        ],
        compiler_params=pltpu.CompilerParams(vmem_limit_bytes=VMEM_BYTES),
        cost_estimate=pl.CostEstimate(flops=10**9, bytes_accessed=0, transcendentals=0),
    )(row_taps, col_taps)


def match_kernel(
    offset, targets_in, quarters_in, rows_in, count_in, pixels, variance, table,
    col_band, row_band, keep_out, send_out,
    targets, quarters, table_rows, count, canvas, total, coefficients, scalar_done, out_done,
):
    side = pixels.shape[1]
    nbasis = col_band.shape[0]
    blocks = pixels.shape[0]
    group, rows, _ = total.shape
    far, start = offset
    where = my_place(canvas.shape[2])
    top = pl.multiple_of((where[4] ^ far) * (side // 2) + start, rows)
    scalars = [
        pltpu.make_async_copy(a, b, scalar_done.at[i])
        for i, (a, b) in enumerate(
            [(targets_in, targets), (quarters_in, quarters), (rows_in, table_rows),
             (count_in, count)]
        )
    ]
    start_all(scalars)
    canvas[...] = jnp.zeros_like(canvas)
    coefficients[:, :, : table.shape[2]] = table[...]
    lane = lax.broadcasted_iota(jnp.int32, (1, side), 1).astype(f32)
    sub = lax.broadcasted_iota(jnp.int32, (8, side), 0).astype(f32)
    step = 8.0 / side
    wait_all(scalars)

    def add_group(j, carry):
        terms = []
        for member in range(group):
            n = group * j + member
            quarter = quarters[n]
            across = (lane + 0.5) / side - 1.0 + lax.rem(quarter, 2).astype(f32)
            down = (sub + 0.5 + top.astype(f32)) / side - 1.0 + (quarter // 2).astype(f32)
            entry = table_rows[n]
            chunk = coefficients[:, :, pl.ds(pl.multiple_of((entry // 128) * 128, 128), 128)]
            chunk = chunk.reshape(-1, 128)
            chunk = pltpu.roll(chunk, lax.rem(128 - lax.rem(entry, 128), 128), 1)
            poly = jnp.broadcast_to(chunk[:, :1], (chunk.shape[0], side))
            poly = [poly[i * nbasis : (i + 1) * nbasis] for i in range(chunk.shape[0] // nbasis)]
            constant = poly[0] + across * (poly[1] + across * poly[3])
            linear = poly[2] + across * poly[4]
            terms.append((constant, linear, poly[5], down))
        left = col_band[:, pl.ds(top, rows), :].reshape(nbasis * rows, 2 * side)
        halves = []
        for pair in range(group // 2):
            n = group * j + 2 * pair
            both = jnp.concatenate([pixels[n], pixels[n + 1]], axis=1)
            right = jnp.concatenate(split_right(both), axis=0)
            convolved = jnp.dot(left, right, preferred_element_type=f32)
            halves.append(split_left(convolved))
        for k in range(nbasis):
            at = slice(k * rows, (k + 1) * rows)
            stacked = []
            for member in range(group):
                first, second = halves[member // 2]
                lanes = slice((member % 2) * side, (member % 2 + 1) * side)
                stacked.append(jnp.concatenate([first[at, lanes], second[at, lanes]], axis=1))
            spread = jnp.dot(
                jnp.concatenate(stacked, axis=0), row_band[k], preferred_element_type=f32
            )
            for member in range(group):
                constant, linear, square, down = terms[member]
                b, d = linear[k : k + 1], square[k : k + 1]
                weight = constant[k : k + 1] + down * (b + down * d)
                change = step * b + d * (2.0 * step * down + step * step)
                second_change = (2.0 * step * step) * d
                for i in range(rows // 8):
                    value = weight * spread[member * rows + 8 * i : member * rows + 8 * i + 8]
                    if k == 0:
                        total[member, 8 * i : 8 * i + 8] = value
                    else:
                        total[member, 8 * i : 8 * i + 8] += value
                    if i < rows // 8 - 1:
                        weight = weight + change
                        change = change + second_change
        for member in range(group):
            n = group * j + member
            live = jnp.where(n < count[0], 1.0, 0.0).astype(f32)
            core, depth, down, across = place_of(where, targets[n], quarters[n])
            column = pl.ds(pl.multiple_of(across * side, side), side)
            canvas[core, down, depth, :, column] += (
                live / variance[n, pl.ds(top, rows), :]
            ) * total[member]
        return carry

    lax.fori_loop(0, blocks // group, add_group, 0)
    outs = [
        pltpu.make_async_copy(canvas.at[1], send_out, out_done.at[0]),
        pltpu.make_async_copy(canvas.at[0], keep_out, out_done.at[1]),
    ]
    start_all(outs)
    wait_all(outs)


def match(
    offset, rows, targets, quarters, table_rows, count, pixels, variance, table,
    col_band, row_band, depths,
):
    blocks, side, _ = pixels.shape
    nbasis = col_band.shape[0]
    group = min(blocks, GROUP_ROWS // rows)
    part = jax.ShapeDtypeStruct((2, depths, rows, 2 * side), f32)
    anywhere = pl.BlockSpec(memory_space=pltpu.HBM)
    vector = pl.BlockSpec(memory_space=pltpu.VMEM)
    entries = -(-table.shape[2] // 128) * 128
    scalars = (targets, quarters, table_rows, count)
    return pl.pallas_call(
        functools.partial(match_kernel, offset),
        out_shape=(part, part),
        in_specs=[anywhere] * 4 + [vector] * 5,
        out_specs=[anywhere] * 2,
        scratch_shapes=[pltpu.SMEM(a.shape, jnp.int32) for a in scalars]
        + [
            pltpu.VMEM((2, 2, depths, rows, 2 * side), f32),
            pltpu.VMEM((group, rows, side), f32),
            pltpu.VMEM(table.shape[:2] + (entries,), f32),
            pltpu.SemaphoreType.DMA((4,)),
            pltpu.SemaphoreType.DMA((2,)),
        ],
        compiler_params=pltpu.CompilerParams(vmem_limit_bytes=VMEM_BYTES),
        cost_estimate=pl.CostEstimate(
            flops=blocks * rows * side * 40960, bytes_accessed=10**7, transcendentals=0
        ),
    )(*scalars, pixels, variance, table, col_band, row_band)


def on_device(
    image, variance, dest_patch, quadrant, coef_index, block_count, coef_table, row_taps, col_taps
):
    pixels = image[0, 0]
    variances = variance[0, 0]
    targets = dest_patch[0, 0]
    quarters = quadrant[0, 0]
    table_rows = coef_index[0, 0]
    count = block_count[0]
    owners = lax.axis_size("patch")
    visits = lax.axis_size("visit")
    depths = owners // 2
    side = pixels.shape[1]
    half = side // 2
    table = jnp.transpose(coef_table, (2, 1, 0))
    together = lax.optimization_barrier

    def over_core(value):
        return lax.ppermute(value, "patch", [(i, i ^ 1) for i in range(owners)])

    def over_visit(value, flip):
        return lax.ppermute(value, "visit", [(i, i ^ flip) for i in range(visits)])

    def over_depth(value, shift):
        if depths & (depths - 1) == 0:
            pairs = [(i, i ^ (2 * shift)) for i in range(owners)]
        else:
            pairs = [(i, (i + 2 * shift) % owners) for i in range(owners)]
        return lax.ppermute(value, "patch", pairs)

    def pieces_of(value):
        order = [depths - 1] + list(range(1, depths - 1))
        return [over_depth(value[s], s) for s in order]

    def run(offset, rows, bands):
        return match(
            offset, rows, targets, quarters, table_rows, count, pixels, variances,
            table, bands[0], bands[1], depths,
        )

    def over_core_parts(value):
        return [over_core(value[y]) for y in range(2)]

    bands = make_bands(row_taps, col_taps, side)
    variances, bands = together((variances, bands))
    keep, send = sum_weights(targets, quarters, count, variances, depths)
    got = over_core(send)
    keep, bands = together((keep, bands))
    keep_far, send_far = run((1, 0), half, bands)
    got_far = over_core_parts(send_far)
    far = keep_far + jnp.stack(got_far)
    far, got = together((far, got))
    far_x = over_visit(far, 1)
    weight_odd, weights = keep[1] + got[1], keep[0] + got[0]
    far, weight_odd, weights, bands = together((far, weight_odd, weights, bands))
    weight_depth = over_depth(weight_odd, 1)
    keep_near, send_near = run((0, 0), half, bands)
    got_near = over_core_parts(send_near)
    keep_near, far_x = together((keep_near, far_x))
    near = [keep_near[y] + far_x[y] for y in range(2)]
    near, got_near = together((near, got_near))
    near = [near[y] + got_near[y] for y in range(2)]
    near, weights = together((near, weights))
    near_y = over_visit(near[1], 2)
    weights = [weights[x] + weight_depth[x] for x in range(2)]
    weight_x = over_visit(weights[1], 1)
    weight_own, near_own = together((weights[0], near[0]))
    weights = [weight_own[y] + weight_x[y] for y in range(2)]
    weight_y = over_visit(weights[1], 2)
    part = near_own + near_y
    pieces = pieces_of(part)
    weight_own, part = together((weights[0], part))
    weights = weight_own + weight_y
    weight_pieces = [over_depth(weights[s], 2 * s) for s in range(1, depths // 2)]
    weighted_sum = functools.reduce(jnp.add, pieces, part[0])
    weighted_sum, weights = together((weighted_sum, weights))
    weight_sum = functools.reduce(jnp.add, weight_pieces, weights[0])
    return weighted_sum[None], weight_sum[None]


def solution(mesh):
    placed = (
        P("visit", "patch", None, None, None),
        P("visit", "patch", None, None, None),
        P("visit", "patch", None),
        P("visit", "patch", None),
        P("visit", "patch", None),
        P("visit", "patch"),
        P(),
        P(),
        P(),
    )
    return jax.shard_map(
        on_device,
        mesh=mesh,
        in_specs=placed,
        out_specs=(P("patch", "visit", None), P("patch", "visit", None)),
        check_vma=False,
    )
```

```python
import functools

import jax
import jax.numpy as jnp
from jax import lax
from jax.experimental import pallas as pl
from jax.experimental.pallas import tpu as pltpu
from jax.sharding import PartitionSpec as P

f32 = jnp.float32
bf16 = jnp.bfloat16

SHARE = 1.0 / 32.0
KEEP = 1.0 - SHARE
VMEM_BYTES = 40 * 2**20
GROUP_ROWS = 1024


def split_left(value):
    first = value.astype(bf16)
    return first, (value - KEEP * first.astype(f32)).astype(bf16)


def split_right(value):
    first = (KEEP * value).astype(bf16)
    return first, ((value - first.astype(f32)) * (1.0 / SHARE)).astype(bf16)


def relative(depth, own, depths):
    if depths & (depths - 1) == 0:
        return depth ^ own
    return lax.rem(depth - own + depths, depths)


def my_place(depths):
    patch_at = lax.axis_index("patch")
    visit_at = lax.axis_index("visit")
    return lax.rem(patch_at, 2), patch_at // 2, depths, visit_at // 2, lax.rem(visit_at, 2)


def place_of(where, target, quarter):
    core = lax.rem(target, 2) ^ where[0]
    depth = relative(target // 2, where[1], where[2])
    return core, depth, (quarter // 2) ^ where[3], lax.rem(quarter, 2)


def start_all(copies):
    for copy in copies:
        copy.start()


def wait_all(copies):
    for copy in copies:
        copy.wait()


def weight_kernel(
    targets_in, quarters_in, count_in, variance_in, keep_out, send_out,
    targets, quarters, count, variance, canvas, scalar_done, block_done, out_done,
):
    blocks, side, _ = variance.shape
    half = side // 2
    chunks = block_done.shape[0]
    size = blocks // chunks
    scalars = [
        pltpu.make_async_copy(a, b, scalar_done.at[i])
        for i, (a, b) in enumerate(
            [(targets_in, targets), (quarters_in, quarters), (count_in, count)]
        )
    ]
    arrays = [
        pltpu.make_async_copy(
            variance_in.at[pl.ds(i * size, size)],
            variance.at[pl.ds(i * size, size)],
            block_done.at[i],
        )
        for i in range(chunks)
    ]
    start_all(scalars)
    start_all(arrays)
    canvas[...] = jnp.zeros_like(canvas)
    where = my_place(2 * canvas.shape[4])
    wait_all(scalars)

    def add_block(n, carry):
        live = jnp.where(n < count[0], 1.0, 0.0).astype(f32)
        inverse = live / variance[n]
        core, depth, down, across = place_of(where, targets[n], quarters[n])
        column = pl.ds(pl.multiple_of(across * side, side), side)
        for part in range(2):
            canvas[
                core, lax.rem(depth, 2), part ^ where[4], down, depth // 2, :, column
            ] += inverse[
                part * half : (part + 1) * half
            ]
        return carry

    for i in range(chunks):
        arrays[i].wait()
        lax.fori_loop(i * size, (i + 1) * size, add_block, 0, unroll=2)
    outs = [
        pltpu.make_async_copy(canvas.at[1], send_out, out_done.at[0]),
        pltpu.make_async_copy(canvas.at[0], keep_out, out_done.at[1]),
    ]
    start_all(outs)
    wait_all(outs)


def sum_weights(targets, quarters, count, variance, depths):
    blocks, side, _ = variance.shape
    half = side // 2
    part = jax.ShapeDtypeStruct((2, 2, 2, depths // 2, half, 2 * side), f32)
    anywhere = pl.BlockSpec(memory_space=pltpu.HBM)
    return pl.pallas_call(
        weight_kernel,
        out_shape=(part, part),
        in_specs=[anywhere] * 4,
        out_specs=[anywhere] * 2,
        scratch_shapes=[
            pltpu.SMEM(targets.shape, jnp.int32),
            pltpu.SMEM(quarters.shape, jnp.int32),
            pltpu.SMEM(count.shape, jnp.int32),
            pltpu.VMEM(variance.shape, f32),
            pltpu.VMEM((2,) + part.shape, f32),
            pltpu.SemaphoreType.DMA((3,)),
            pltpu.SemaphoreType.DMA((4,)),
            pltpu.SemaphoreType.DMA((2,)),
        ],
        compiler_params=pltpu.CompilerParams(vmem_limit_bytes=VMEM_BYTES),
        cost_estimate=pl.CostEstimate(flops=10**9, bytes_accessed=0, transcendentals=0),
    )(targets, quarters, count, variance)


def band_kernel(
    row_taps_in, col_taps_in, col_out, row_out, row_padded, col_padded, col_band, row_band, done
):
    nbasis, taps = row_taps_in.shape
    side = row_padded.shape[1]
    radius = (taps - 1) // 2
    row_padded[...] = jnp.zeros_like(row_padded)
    col_padded[...] = jnp.zeros_like(col_padded)
    row_padded[:, :taps] = row_taps_in[...]
    col_padded[:, :taps] = col_taps_in[...]
    row = lax.broadcasted_iota(jnp.int32, (side, side), 0)
    column = lax.broadcasted_iota(jnp.int32, (side, side), 1)
    near = jnp.abs(row - column) <= radius
    row_placed = pltpu.roll(row_padded[...], side - radius, 1)
    turn = (lax.rem(column - radius + row + side, side) == 0).astype(f32)
    col_placed = jnp.dot(
        col_padded[...], turn, precision=lax.Precision.HIGHEST, preferred_element_type=f32
    )
    for k in range(nbasis):
        base = jnp.broadcast_to(col_placed[k : k + 1], (side, side))
        band = jnp.where(near, pltpu.roll(base, 0, 1, stride=1, stride_axis=0), 0.0)
        first, second = split_left(band)
        col_band[k, :, :side] = first
        col_band[k, :, side:] = second
    col_copy = pltpu.make_async_copy(col_band, col_out, done.at[0])
    col_copy.start()
    for k in range(nbasis):
        base = jnp.broadcast_to(row_placed[k : k + 1], (side, side))
        band = jnp.where(near, pltpu.roll(base, 0, 1, stride=1, stride_axis=0), 0.0)
        first, second = split_right(band)
        row_band[k, :side, :] = first
        row_band[k, side:, :] = second
    row_copy = pltpu.make_async_copy(row_band, row_out, done.at[1])
    row_copy.start()
    col_copy.wait()
    row_copy.wait()


def make_bands(row_taps, col_taps, side):
    nbasis, taps = row_taps.shape
    anywhere = pl.BlockSpec(memory_space=pltpu.HBM)
    col_shape, row_shape = (nbasis, side, 2 * side), (nbasis, 2 * side, side)
    tap_block = pl.BlockSpec((nbasis, taps), lambda i: (0, 0))
    return pl.pallas_call(
        band_kernel,
        grid=(1,),
        out_shape=(
            jax.ShapeDtypeStruct(col_shape, bf16),
            jax.ShapeDtypeStruct(row_shape, bf16),
        ),
        in_specs=[tap_block] * 2,
        out_specs=[anywhere] * 2,
        scratch_shapes=[
            pltpu.VMEM((nbasis, side), f32),
            pltpu.VMEM((nbasis, side), f32),
            pltpu.VMEM(col_shape, bf16),
            pltpu.VMEM(row_shape, bf16),
            pltpu.SemaphoreType.DMA((2,)),
        ],
        compiler_params=pltpu.CompilerParams(vmem_limit_bytes=VMEM_BYTES),
        cost_estimate=pl.CostEstimate(flops=10**9, bytes_accessed=0, transcendentals=0),
    )(row_taps, col_taps)


def match_kernel(
    offset, targets_in, quarters_in, rows_in, count_in, pixels, variance, table,
    col_band, row_band, keep_out, send_out,
    targets, quarters, table_rows, count, canvas, total, coefficients, scalar_done, out_done,
):
    side = pixels.shape[1]
    nbasis = col_band.shape[0]
    blocks = pixels.shape[0]
    group, rows, _ = total.shape
    far, start = offset
    where = my_place(canvas.shape[2])
    top = pl.multiple_of((where[4] ^ far) * (side // 2) + start, rows)
    scalars = [
        pltpu.make_async_copy(a, b, scalar_done.at[i])
        for i, (a, b) in enumerate(
            [(targets_in, targets), (quarters_in, quarters), (rows_in, table_rows),
             (count_in, count)]
        )
    ]
    start_all(scalars)
    canvas[...] = jnp.zeros_like(canvas)
    coefficients[:, :, : table.shape[2]] = table[...]
    lane = lax.broadcasted_iota(jnp.int32, (1, side), 1).astype(f32)
    sub = lax.broadcasted_iota(jnp.int32, (8, side), 0).astype(f32)
    step = 8.0 / side
    wait_all(scalars)

    def add_group(j, carry):
        terms = []
        for member in range(group):
            n = group * j + member
            quarter = quarters[n]
            across = (lane + 0.5) / side - 1.0 + lax.rem(quarter, 2).astype(f32)
            down = (sub + 0.5 + top.astype(f32)) / side - 1.0 + (quarter // 2).astype(f32)
            entry = table_rows[n]
            chunk = coefficients[:, :, pl.ds(pl.multiple_of((entry // 128) * 128, 128), 128)]
            chunk = chunk.reshape(-1, 128)
            chunk = pltpu.roll(chunk, lax.rem(128 - lax.rem(entry, 128), 128), 1)
            poly = jnp.broadcast_to(chunk[:, :1], (chunk.shape[0], side))
            poly = [poly[i * nbasis : (i + 1) * nbasis] for i in range(chunk.shape[0] // nbasis)]
            constant = poly[0] + across * (poly[1] + across * poly[3])
            linear = poly[2] + across * poly[4]
            terms.append((constant, linear, poly[5], down))
        left = col_band[:, pl.ds(top, rows), :].reshape(nbasis * rows, 2 * side)
        halves = []
        for pair in range(group // 2):
            n = group * j + 2 * pair
            both = jnp.concatenate([pixels[n], pixels[n + 1]], axis=1)
            right = jnp.concatenate(split_right(both), axis=0)
            convolved = jnp.dot(left, right, preferred_element_type=f32)
            halves.append(split_left(convolved))
        for k in range(nbasis):
            at = slice(k * rows, (k + 1) * rows)
            stacked = []
            for member in range(group):
                first, second = halves[member // 2]
                lanes = slice((member % 2) * side, (member % 2 + 1) * side)
                stacked.append(jnp.concatenate([first[at, lanes], second[at, lanes]], axis=1))
            spread = jnp.dot(
                jnp.concatenate(stacked, axis=0), row_band[k], preferred_element_type=f32
            )
            for member in range(group):
                constant, linear, square, down = terms[member]
                b, d = linear[k : k + 1], square[k : k + 1]
                weight = constant[k : k + 1] + down * (b + down * d)
                change = step * b + d * (2.0 * step * down + step * step)
                second_change = (2.0 * step * step) * d
                for i in range(rows // 8):
                    value = weight * spread[member * rows + 8 * i : member * rows + 8 * i + 8]
                    if k == 0:
                        total[member, 8 * i : 8 * i + 8] = value
                    else:
                        total[member, 8 * i : 8 * i + 8] += value
                    if i < rows // 8 - 1:
                        weight = weight + change
                        change = change + second_change
        for member in range(group):
            n = group * j + member
            live = jnp.where(n < count[0], 1.0, 0.0).astype(f32)
            core, depth, down, across = place_of(where, targets[n], quarters[n])
            column = pl.ds(pl.multiple_of(across * side, side), side)
            canvas[core, down, depth, :, column] += (
                live / variance[n, pl.ds(top, rows), :]
            ) * total[member]
        return carry

    lax.fori_loop(0, blocks // group, add_group, 0)
    outs = [
        pltpu.make_async_copy(canvas.at[1], send_out, out_done.at[0]),
        pltpu.make_async_copy(canvas.at[0], keep_out, out_done.at[1]),
    ]
    start_all(outs)
    wait_all(outs)


def match(
    offset, rows, targets, quarters, table_rows, count, pixels, variance, table,
    col_band, row_band, depths,
):
    blocks, side, _ = pixels.shape
    nbasis = col_band.shape[0]
    group = min(blocks, GROUP_ROWS // rows)
    part = jax.ShapeDtypeStruct((2, depths, rows, 2 * side), f32)
    anywhere = pl.BlockSpec(memory_space=pltpu.HBM)
    vector = pl.BlockSpec(memory_space=pltpu.VMEM)
    entries = -(-table.shape[2] // 128) * 128
    scalars = (targets, quarters, table_rows, count)
    return pl.pallas_call(
        functools.partial(match_kernel, offset),
        out_shape=(part, part),
        in_specs=[anywhere] * 4 + [vector] * 5,
        out_specs=[anywhere] * 2,
        scratch_shapes=[pltpu.SMEM(a.shape, jnp.int32) for a in scalars]
        + [
            pltpu.VMEM((2, 2, depths, rows, 2 * side), f32),
            pltpu.VMEM((group, rows, side), f32),
            pltpu.VMEM(table.shape[:2] + (entries,), f32),
            pltpu.SemaphoreType.DMA((4,)),
            pltpu.SemaphoreType.DMA((2,)),
        ],
        compiler_params=pltpu.CompilerParams(vmem_limit_bytes=VMEM_BYTES),
        cost_estimate=pl.CostEstimate(
            flops=blocks * rows * side * 40960, bytes_accessed=10**7, transcendentals=0
        ),
    )(*scalars, pixels, variance, table, col_band, row_band)


def on_device(
    image, variance, dest_patch, quadrant, coef_index, block_count, coef_table, row_taps, col_taps
):
    pixels = image[0, 0]
    variances = variance[0, 0]
    targets = dest_patch[0, 0]
    quarters = quadrant[0, 0]
    table_rows = coef_index[0, 0]
    count = block_count[0]
    owners = lax.axis_size("patch")
    visits = lax.axis_size("visit")
    depths = owners // 2
    side = pixels.shape[1]
    half = side // 2
    table = jnp.transpose(coef_table, (2, 1, 0))
    together = lax.optimization_barrier

    def over_core(value):
        return lax.ppermute(value, "patch", [(i, i ^ 1) for i in range(owners)])

    def over_visit(value, flip):
        return lax.ppermute(value, "visit", [(i, i ^ flip) for i in range(visits)])

    def over_depth(value, shift):
        if depths & (depths - 1) == 0:
            pairs = [(i, i ^ (2 * shift)) for i in range(owners)]
        else:
            pairs = [(i, (i + 2 * shift) % owners) for i in range(owners)]
        return lax.ppermute(value, "patch", pairs)

    def pieces_of(value):
        order = [depths - 1] + list(range(1, depths - 1))
        return [over_depth(value[s], s) for s in order]

    def run(offset, rows, bands):
        return match(
            offset, rows, targets, quarters, table_rows, count, pixels, variances,
            table, bands[0], bands[1], depths,
        )

    def over_core_parts(value):
        return [over_core(value[y]) for y in range(2)]

    bands = make_bands(row_taps, col_taps, side)
    variances, bands = together((variances, bands))
    keep, send = sum_weights(targets, quarters, count, variances, depths)
    got = over_core(send)
    keep, bands = together((keep, bands))
    keep_far, send_far = run((1, 0), half, bands)
    got_far = over_core_parts(send_far)
    far = keep_far + jnp.stack(got_far)
    far, got = together((far, got))
    far_x = over_visit(far, 1)
    weight_odd, weights = keep[1] + got[1], keep[0] + got[0]
    far, weight_odd, weights, bands = together((far, weight_odd, weights, bands))
    weight_depth = over_depth(weight_odd, 1)
    keep_near, send_near = run((0, 0), half, bands)
    got_near = over_core_parts(send_near)
    keep_near, far_x = together((keep_near, far_x))
    near = [keep_near[y] + far_x[y] for y in range(2)]
    near, got_near = together((near, got_near))
    near = [near[y] + got_near[y] for y in range(2)]
    near, weights = together((near, weights))
    near_y = over_visit(near[1], 2)
    weights = [weights[x] + weight_depth[x] for x in range(2)]
    weight_x = over_visit(weights[1], 1)
    weight_own, near_own = together((weights[0], near[0]))
    weights = [weight_own[y] + weight_x[y] for y in range(2)]
    weight_y = over_visit(weights[1], 2)
    part = near_own + near_y
    pieces = pieces_of(part)
    weight_own, part = together((weights[0], part))
    weights = weight_own + weight_y
    weight_pieces = [over_depth(weights[s], 2 * s) for s in range(1, depths // 2)]
    weighted_sum = functools.reduce(jnp.add, pieces, part[0])
    weighted_sum, weights = together((weighted_sum, weights))
    weight_sum = functools.reduce(jnp.add, weight_pieces, weights[0])
    return weighted_sum[None], weight_sum[None]


def solution(mesh):
    placed = (
        P("visit", "patch", None, None, None),
        P("visit", "patch", None, None, None),
        P("visit", "patch", None),
        P("visit", "patch", None),
        P("visit", "patch", None),
        P("visit", "patch"),
        P(),
        P(),
        P(),
    )
    return jax.shard_map(
        on_device,
        mesh=mesh,
        in_specs=placed,
        out_specs=(P("patch", "visit", None), P("patch", "visit", None)),
        check_vma=False,
    )
```

```python
import functools

import jax
import jax.numpy as jnp
from jax import lax
from jax.experimental import pallas as pl
from jax.experimental.pallas import tpu as pltpu
from jax.sharding import PartitionSpec as P

f32 = jnp.float32
bf16 = jnp.bfloat16

SHARE = 1.0 / 32.0
KEEP = 1.0 - SHARE
VMEM_BYTES = 40 * 2**20
GROUP_ROWS = 1024


def split_left(value):
    first = value.astype(bf16)
    return first, (value - KEEP * first.astype(f32)).astype(bf16)


def split_right(value):
    first = (KEEP * value).astype(bf16)
    return first, ((value - first.astype(f32)) * (1.0 / SHARE)).astype(bf16)


def relative(depth, own, depths):
    if depths & (depths - 1) == 0:
        return depth ^ own
    return lax.rem(depth - own + depths, depths)


def my_place(depths):
    patch_at = lax.axis_index("patch")
    visit_at = lax.axis_index("visit")
    return lax.rem(patch_at, 2), patch_at // 2, depths, visit_at // 2, lax.rem(visit_at, 2)


def place_of(where, target, quarter):
    core = lax.rem(target, 2) ^ where[0]
    depth = relative(target // 2, where[1], where[2])
    return core, depth, (quarter // 2) ^ where[3], lax.rem(quarter, 2)


def start_all(copies):
    for copy in copies:
        copy.start()


def wait_all(copies):
    for copy in copies:
        copy.wait()


def weight_kernel(
    targets_in, quarters_in, count_in, variance_in, keep_out, send_out,
    targets, quarters, count, variance, canvas, scalar_done, block_done, out_done,
):
    blocks, side, _ = variance.shape
    half = side // 2
    chunks = block_done.shape[0]
    size = blocks // chunks
    scalars = [
        pltpu.make_async_copy(a, b, scalar_done.at[i])
        for i, (a, b) in enumerate(
            [(targets_in, targets), (quarters_in, quarters), (count_in, count)]
        )
    ]
    arrays = [
        pltpu.make_async_copy(
            variance_in.at[pl.ds(i * size, size)],
            variance.at[pl.ds(i * size, size)],
            block_done.at[i],
        )
        for i in range(chunks)
    ]
    start_all(scalars)
    start_all(arrays)
    canvas[...] = jnp.zeros_like(canvas)
    where = my_place(2 * canvas.shape[4])
    wait_all(scalars)

    def add_block(n, carry):
        live = jnp.where(n < count[0], 1.0, 0.0).astype(f32)
        inverse = live / variance[n]
        core, depth, down, across = place_of(where, targets[n], quarters[n])
        column = pl.ds(pl.multiple_of(across * side, side), side)
        for part in range(2):
            canvas[
                core, lax.rem(depth, 2), part ^ where[4], down, depth // 2, :, column
            ] += inverse[
                part * half : (part + 1) * half
            ]
        return carry

    for i in range(chunks):
        arrays[i].wait()
        lax.fori_loop(i * size, (i + 1) * size, add_block, 0, unroll=2)
    outs = [
        pltpu.make_async_copy(canvas.at[1], send_out, out_done.at[0]),
        pltpu.make_async_copy(canvas.at[0], keep_out, out_done.at[1]),
    ]
    start_all(outs)
    wait_all(outs)


def sum_weights(targets, quarters, count, variance, depths):
    blocks, side, _ = variance.shape
    half = side // 2
    part = jax.ShapeDtypeStruct((2, 2, 2, depths // 2, half, 2 * side), f32)
    anywhere = pl.BlockSpec(memory_space=pltpu.HBM)
    return pl.pallas_call(
        weight_kernel,
        out_shape=(part, part),
        in_specs=[anywhere] * 4,
        out_specs=[anywhere] * 2,
        scratch_shapes=[
            pltpu.SMEM(targets.shape, jnp.int32),
            pltpu.SMEM(quarters.shape, jnp.int32),
            pltpu.SMEM(count.shape, jnp.int32),
            pltpu.VMEM(variance.shape, f32),
            pltpu.VMEM((2,) + part.shape, f32),
            pltpu.SemaphoreType.DMA((3,)),
            pltpu.SemaphoreType.DMA((4,)),
            pltpu.SemaphoreType.DMA((2,)),
        ],
        compiler_params=pltpu.CompilerParams(vmem_limit_bytes=VMEM_BYTES),
        cost_estimate=pl.CostEstimate(flops=10**9, bytes_accessed=0, transcendentals=0),
    )(targets, quarters, count, variance)


def band_kernel(
    taps_in, col_out, row_out, row_padded, col_padded, col_band, row_band, done
):
    nbasis, taps = row_padded.shape[0], taps_in.shape[1]
    side = row_padded.shape[1]
    radius = (taps - 1) // 2
    row_padded[...] = jnp.zeros_like(row_padded)
    col_padded[...] = jnp.zeros_like(col_padded)
    row_padded[:, :taps] = taps_in[:nbasis]
    col_padded[:, :taps] = taps_in[nbasis:]
    row = lax.broadcasted_iota(jnp.int32, (side, side), 0)
    column = lax.broadcasted_iota(jnp.int32, (side, side), 1)
    near = jnp.abs(row - column) <= radius
    row_placed = pltpu.roll(row_padded[...], side - radius, 1)
    turn = (lax.rem(column - radius + row + side, side) == 0).astype(f32)
    col_placed = jnp.dot(
        col_padded[...], turn, precision=lax.Precision.HIGHEST, preferred_element_type=f32
    )
    for k in range(nbasis):
        base = jnp.broadcast_to(col_placed[k : k + 1], (side, side))
        band = jnp.where(near, pltpu.roll(base, 0, 1, stride=1, stride_axis=0), 0.0)
        first, second = split_left(band)
        col_band[k, :, :side] = first
        col_band[k, :, side:] = second
    col_copy = pltpu.make_async_copy(col_band, col_out, done.at[0])
    col_copy.start()
    for k in range(nbasis):
        base = jnp.broadcast_to(row_placed[k : k + 1], (side, side))
        band = jnp.where(near, pltpu.roll(base, 0, 1, stride=1, stride_axis=0), 0.0)
        first, second = split_right(band)
        row_band[k, :side, :] = first
        row_band[k, side:, :] = second
    row_copy = pltpu.make_async_copy(row_band, row_out, done.at[1])
    row_copy.start()
    col_copy.wait()
    row_copy.wait()


def make_bands(row_taps, col_taps, side):
    nbasis, taps = row_taps.shape
    anywhere = pl.BlockSpec(memory_space=pltpu.HBM)
    col_shape, row_shape = (nbasis, side, 2 * side), (nbasis, 2 * side, side)
    tap_block = pl.BlockSpec((2 * nbasis, taps), lambda i: (0, 0))
    return pl.pallas_call(
        band_kernel,
        grid=(1,),
        out_shape=(
            jax.ShapeDtypeStruct(col_shape, bf16),
            jax.ShapeDtypeStruct(row_shape, bf16),
        ),
        in_specs=[tap_block],
        out_specs=[anywhere] * 2,
        scratch_shapes=[
            pltpu.VMEM((nbasis, side), f32),
            pltpu.VMEM((nbasis, side), f32),
            pltpu.VMEM(col_shape, bf16),
            pltpu.VMEM(row_shape, bf16),
            pltpu.SemaphoreType.DMA((2,)),
        ],
        compiler_params=pltpu.CompilerParams(vmem_limit_bytes=VMEM_BYTES),
        cost_estimate=pl.CostEstimate(flops=10**9, bytes_accessed=0, transcendentals=0),
    )(jnp.concatenate([row_taps, col_taps], axis=0))


def match_kernel(
    offset, targets_in, quarters_in, rows_in, count_in, pixels, variance, table,
    col_band, row_band, keep_out, send_out,
    targets, quarters, table_rows, count, canvas, total, coefficients, scalar_done, out_done,
):
    side = pixels.shape[1]
    nbasis = col_band.shape[0]
    blocks = pixels.shape[0]
    group, rows, _ = total.shape
    far, start = offset
    where = my_place(canvas.shape[2])
    top = pl.multiple_of((where[4] ^ far) * (side // 2) + start, rows)
    scalars = [
        pltpu.make_async_copy(a, b, scalar_done.at[i])
        for i, (a, b) in enumerate(
            [(targets_in, targets), (quarters_in, quarters), (rows_in, table_rows),
             (count_in, count)]
        )
    ]
    start_all(scalars)
    canvas[...] = jnp.zeros_like(canvas)
    coefficients[:, :, : table.shape[2]] = table[...]
    lane = lax.broadcasted_iota(jnp.int32, (1, side), 1).astype(f32)
    sub = lax.broadcasted_iota(jnp.int32, (8, side), 0).astype(f32)
    step = 8.0 / side
    wait_all(scalars)

    def add_group(j, carry):
        terms = []
        for member in range(group):
            n = group * j + member
            quarter = quarters[n]
            across = (lane + 0.5) / side - 1.0 + lax.rem(quarter, 2).astype(f32)
            down = (sub + 0.5 + top.astype(f32)) / side - 1.0 + (quarter // 2).astype(f32)
            entry = table_rows[n]
            chunk = coefficients[:, :, pl.ds(pl.multiple_of((entry // 128) * 128, 128), 128)]
            chunk = chunk.reshape(-1, 128)
            chunk = pltpu.roll(chunk, lax.rem(128 - lax.rem(entry, 128), 128), 1)
            poly = jnp.broadcast_to(chunk[:, :1], (chunk.shape[0], side))
            poly = [poly[i * nbasis : (i + 1) * nbasis] for i in range(chunk.shape[0] // nbasis)]
            constant = poly[0] + across * (poly[1] + across * poly[3])
            linear = poly[2] + across * poly[4]
            terms.append((constant, linear, poly[5], down))
        left = col_band[:, pl.ds(top, rows), :].reshape(nbasis * rows, 2 * side)
        halves = []
        for pair in range(group // 2):
            n = group * j + 2 * pair
            both = jnp.concatenate([pixels[n], pixels[n + 1]], axis=1)
            right = jnp.concatenate(split_right(both), axis=0)
            convolved = jnp.dot(left, right, preferred_element_type=f32)
            halves.append(split_left(convolved))
        for k in range(nbasis):
            at = slice(k * rows, (k + 1) * rows)
            stacked = []
            for member in range(group):
                first, second = halves[member // 2]
                lanes = slice((member % 2) * side, (member % 2 + 1) * side)
                stacked.append(jnp.concatenate([first[at, lanes], second[at, lanes]], axis=1))
            spread = jnp.dot(
                jnp.concatenate(stacked, axis=0), row_band[k], preferred_element_type=f32
            )
            for member in range(group):
                constant, linear, square, down = terms[member]
                b, d = linear[k : k + 1], square[k : k + 1]
                weight = constant[k : k + 1] + down * (b + down * d)
                change = step * b + d * (2.0 * step * down + step * step)
                second_change = (2.0 * step * step) * d
                for i in range(rows // 8):
                    value = weight * spread[member * rows + 8 * i : member * rows + 8 * i + 8]
                    if k == 0:
                        total[member, 8 * i : 8 * i + 8] = value
                    else:
                        total[member, 8 * i : 8 * i + 8] += value
                    if i < rows // 8 - 1:
                        weight = weight + change
                        change = change + second_change
        for member in range(group):
            n = group * j + member
            live = jnp.where(n < count[0], 1.0, 0.0).astype(f32)
            core, depth, down, across = place_of(where, targets[n], quarters[n])
            column = pl.ds(pl.multiple_of(across * side, side), side)
            canvas[core, down, depth, :, column] += (
                live / variance[n, pl.ds(top, rows), :]
            ) * total[member]
        return carry

    lax.fori_loop(0, blocks // group, add_group, 0)
    outs = [
        pltpu.make_async_copy(canvas.at[1], send_out, out_done.at[0]),
        pltpu.make_async_copy(canvas.at[0], keep_out, out_done.at[1]),
    ]
    start_all(outs)
    wait_all(outs)


def match(
    offset, rows, targets, quarters, table_rows, count, pixels, variance, table,
    col_band, row_band, depths,
):
    blocks, side, _ = pixels.shape
    nbasis = col_band.shape[0]
    group = min(blocks, GROUP_ROWS // rows)
    part = jax.ShapeDtypeStruct((2, depths, rows, 2 * side), f32)
    anywhere = pl.BlockSpec(memory_space=pltpu.HBM)
    vector = pl.BlockSpec(memory_space=pltpu.VMEM)
    entries = -(-table.shape[2] // 128) * 128
    scalars = (targets, quarters, table_rows, count)
    return pl.pallas_call(
        functools.partial(match_kernel, offset),
        out_shape=(part, part),
        in_specs=[anywhere] * 4 + [vector] * 5,
        out_specs=[anywhere] * 2,
        scratch_shapes=[pltpu.SMEM(a.shape, jnp.int32) for a in scalars]
        + [
            pltpu.VMEM((2, 2, depths, rows, 2 * side), f32),
            pltpu.VMEM((group, rows, side), f32),
            pltpu.VMEM(table.shape[:2] + (entries,), f32),
            pltpu.SemaphoreType.DMA((4,)),
            pltpu.SemaphoreType.DMA((2,)),
        ],
        compiler_params=pltpu.CompilerParams(vmem_limit_bytes=VMEM_BYTES),
        cost_estimate=pl.CostEstimate(
            flops=blocks * rows * side * 40960, bytes_accessed=10**7, transcendentals=0
        ),
    )(*scalars, pixels, variance, table, col_band, row_band)


def on_device(
    image, variance, dest_patch, quadrant, coef_index, block_count, coef_table, row_taps, col_taps
):
    pixels = image[0, 0]
    variances = variance[0, 0]
    targets = dest_patch[0, 0]
    quarters = quadrant[0, 0]
    table_rows = coef_index[0, 0]
    count = block_count[0]
    owners = lax.axis_size("patch")
    visits = lax.axis_size("visit")
    depths = owners // 2
    side = pixels.shape[1]
    half = side // 2
    table = jnp.transpose(coef_table, (2, 1, 0))
    together = lax.optimization_barrier

    def over_core(value):
        return lax.ppermute(value, "patch", [(i, i ^ 1) for i in range(owners)])

    def over_visit(value, flip):
        return lax.ppermute(value, "visit", [(i, i ^ flip) for i in range(visits)])

    def over_depth(value, shift):
        if depths & (depths - 1) == 0:
            pairs = [(i, i ^ (2 * shift)) for i in range(owners)]
        else:
            pairs = [(i, (i + 2 * shift) % owners) for i in range(owners)]
        return lax.ppermute(value, "patch", pairs)

    def pieces_of(value):
        order = [depths - 1] + list(range(1, depths - 1))
        return [over_depth(value[s], s) for s in order]

    def run(offset, rows, bands):
        return match(
            offset, rows, targets, quarters, table_rows, count, pixels, variances,
            table, bands[0], bands[1], depths,
        )

    def over_core_parts(value):
        return [over_core(value[y]) for y in range(2)]

    bands = make_bands(row_taps, col_taps, side)
    variances, bands = together((variances, bands))
    keep, send = sum_weights(targets, quarters, count, variances, depths)
    got = over_core(send)
    keep, bands = together((keep, bands))
    keep_far, send_far = run((1, 0), half, bands)
    got_far = over_core_parts(send_far)
    far = keep_far + jnp.stack(got_far)
    far, got = together((far, got))
    far_x = over_visit(far, 1)
    weight_odd, weights = keep[1] + got[1], keep[0] + got[0]
    far, weight_odd, weights, bands = together((far, weight_odd, weights, bands))
    weight_depth = over_depth(weight_odd, 1)
    keep_near, send_near = run((0, 0), half, bands)
    got_near = over_core_parts(send_near)
    keep_near, far_x = together((keep_near, far_x))
    near = [keep_near[y] + far_x[y] for y in range(2)]
    near, got_near = together((near, got_near))
    near = [near[y] + got_near[y] for y in range(2)]
    near_y = over_visit(near[1], 2)
    weights = [weights[x] + weight_depth[x] for x in range(2)]
    weight_x = over_visit(weights[1], 1)
    weight_own, near_own = together((weights[0], near[0]))
    weights = [weight_own[y] + weight_x[y] for y in range(2)]
    weight_y = over_visit(weights[1], 2)
    part = near_own + near_y
    pieces = pieces_of(part)
    weight_own, part = together((weights[0], part))
    weights = weight_own + weight_y
    weight_pieces = [over_depth(weights[s], 2 * s) for s in range(1, depths // 2)]
    weighted_sum = functools.reduce(jnp.add, pieces, part[0])
    weighted_sum, weights = together((weighted_sum, weights))
    weight_sum = functools.reduce(jnp.add, weight_pieces, weights[0])
    return weighted_sum[None], weight_sum[None]


def solution(mesh):
    placed = (
        P("visit", "patch", None, None, None),
        P("visit", "patch", None, None, None),
        P("visit", "patch", None),
        P("visit", "patch", None),
        P("visit", "patch", None),
        P("visit", "patch"),
        P(),
        P(),
        P(),
    )
    return jax.shard_map(
        on_device,
        mesh=mesh,
        in_specs=placed,
        out_specs=(P("patch", "visit", None), P("patch", "visit", None)),
        check_vma=False,
    )
```

```python
import functools

import jax
import jax.numpy as jnp
from jax import lax
from jax.experimental import pallas as pl
from jax.experimental.pallas import tpu as pltpu
from jax.sharding import PartitionSpec as P

f32 = jnp.float32
bf16 = jnp.bfloat16

SHARE = 1.0 / 32.0
KEEP = 1.0 - SHARE
VMEM_BYTES = 40 * 2**20
GROUP_ROWS = 1024


def split_left(value):
    first = value.astype(bf16)
    return first, (value - KEEP * first.astype(f32)).astype(bf16)


def split_right(value):
    first = (KEEP * value).astype(bf16)
    return first, ((value - first.astype(f32)) * (1.0 / SHARE)).astype(bf16)


def relative(depth, own, depths):
    if depths & (depths - 1) == 0:
        return depth ^ own
    return lax.rem(depth - own + depths, depths)


def my_place(depths):
    patch_at = lax.axis_index("patch")
    visit_at = lax.axis_index("visit")
    return lax.rem(patch_at, 2), patch_at // 2, depths, visit_at // 2, lax.rem(visit_at, 2)


def place_of(where, target, quarter):
    core = lax.rem(target, 2) ^ where[0]
    depth = relative(target // 2, where[1], where[2])
    return core, depth, (quarter // 2) ^ where[3], lax.rem(quarter, 2)


def start_all(copies):
    for copy in copies:
        copy.start()


def wait_all(copies):
    for copy in copies:
        copy.wait()


def weight_kernel(
    targets_in, quarters_in, count_in, variance, keep_out, send_out,
    targets, quarters, count, canvas, scalar_done, out_done,
):
    blocks, side, _ = variance.shape
    half = side // 2
    scalars = [
        pltpu.make_async_copy(a, b, scalar_done.at[i])
        for i, (a, b) in enumerate(
            [(targets_in, targets), (quarters_in, quarters), (count_in, count)]
        )
    ]
    start_all(scalars)
    canvas[...] = jnp.zeros_like(canvas)
    where = my_place(2 * canvas.shape[4])
    wait_all(scalars)

    def add_block(n, carry):
        live = jnp.where(n < count[0], 1.0, 0.0).astype(f32)
        inverse = live / variance[n]
        core, depth, down, across = place_of(where, targets[n], quarters[n])
        column = pl.ds(pl.multiple_of(across * side, side), side)
        for part in range(2):
            canvas[
                core, lax.rem(depth, 2), part ^ where[4], down, depth // 2, :, column
            ] += inverse[
                part * half : (part + 1) * half
            ]
        return carry

    lax.fori_loop(0, blocks, add_block, 0, unroll=4)
    outs = [
        pltpu.make_async_copy(canvas.at[1], send_out, out_done.at[0]),
        pltpu.make_async_copy(canvas.at[0], keep_out, out_done.at[1]),
    ]
    start_all(outs)
    wait_all(outs)


def sum_weights(targets, quarters, count, variance, depths):
    blocks, side, _ = variance.shape
    half = side // 2
    part = jax.ShapeDtypeStruct((2, 2, 2, depths // 2, half, 2 * side), f32)
    anywhere = pl.BlockSpec(memory_space=pltpu.HBM)
    return pl.pallas_call(
        weight_kernel,
        out_shape=(part, part),
        in_specs=[anywhere] * 3 + [pl.BlockSpec(memory_space=pltpu.VMEM)],
        out_specs=[anywhere] * 2,
        scratch_shapes=[
            pltpu.SMEM(targets.shape, jnp.int32),
            pltpu.SMEM(quarters.shape, jnp.int32),
            pltpu.SMEM(count.shape, jnp.int32),
            pltpu.VMEM((2,) + part.shape, f32),
            pltpu.SemaphoreType.DMA((3,)),
            pltpu.SemaphoreType.DMA((2,)),
        ],
        compiler_params=pltpu.CompilerParams(vmem_limit_bytes=VMEM_BYTES),
        cost_estimate=pl.CostEstimate(flops=10**9, bytes_accessed=0, transcendentals=0),
    )(targets, quarters, count, variance)


def band_kernel(
    taps_in, col_band, row_band, row_padded, col_padded
):
    nbasis, taps = row_padded.shape[0], taps_in.shape[1]
    side = row_padded.shape[1]
    radius = (taps - 1) // 2
    row_padded[...] = jnp.zeros_like(row_padded)
    col_padded[...] = jnp.zeros_like(col_padded)
    row_padded[:, :taps] = taps_in[:nbasis]
    col_padded[:, :taps] = taps_in[nbasis:]
    row = lax.broadcasted_iota(jnp.int32, (side, side), 0)
    column = lax.broadcasted_iota(jnp.int32, (side, side), 1)
    near = jnp.abs(row - column) <= radius
    row_placed = pltpu.roll(row_padded[...], side - radius, 1)
    turn = (lax.rem(column - radius + row + side, side) == 0).astype(f32)
    col_placed = jnp.dot(
        col_padded[...], turn, precision=lax.Precision.HIGHEST, preferred_element_type=f32
    )
    for k in range(nbasis):
        base = jnp.broadcast_to(col_placed[k : k + 1], (side, side))
        band = jnp.where(near, pltpu.roll(base, 0, 1, stride=1, stride_axis=0), 0.0)
        first, second = split_left(band)
        col_band[k, :, :side] = first
        col_band[k, :, side:] = second
    for k in range(nbasis):
        base = jnp.broadcast_to(row_placed[k : k + 1], (side, side))
        band = jnp.where(near, pltpu.roll(base, 0, 1, stride=1, stride_axis=0), 0.0)
        first, second = split_right(band)
        row_band[k, :side, :] = first
        row_band[k, side:, :] = second


def make_bands(row_taps, col_taps, side):
    nbasis, taps = row_taps.shape
    vector = pl.BlockSpec(memory_space=pltpu.VMEM)
    col_shape, row_shape = (nbasis, side, 2 * side), (nbasis, 2 * side, side)
    tap_block = pl.BlockSpec((2 * nbasis, taps), lambda i: (0, 0))
    return pl.pallas_call(
        band_kernel,
        grid=(1,),
        out_shape=(
            jax.ShapeDtypeStruct(col_shape, bf16),
            jax.ShapeDtypeStruct(row_shape, bf16),
        ),
        in_specs=[tap_block],
        out_specs=[vector] * 2,
        scratch_shapes=[
            pltpu.VMEM((nbasis, side), f32),
            pltpu.VMEM((nbasis, side), f32),
        ],
        compiler_params=pltpu.CompilerParams(vmem_limit_bytes=VMEM_BYTES),
        cost_estimate=pl.CostEstimate(flops=10**9, bytes_accessed=0, transcendentals=0),
    )(jnp.concatenate([row_taps, col_taps], axis=0))


def match_kernel(
    offset, targets_in, quarters_in, rows_in, count_in, pixels, variance, table,
    col_band, row_band, keep_out, send_out,
    targets, quarters, table_rows, count, canvas, total, coefficients, scalar_done, out_done,
):
    side = pixels.shape[1]
    nbasis = col_band.shape[0]
    blocks = pixels.shape[0]
    group, rows, _ = total.shape
    far, start = offset
    where = my_place(canvas.shape[2])
    top = pl.multiple_of((where[4] ^ far) * (side // 2) + start, rows)
    scalars = [
        pltpu.make_async_copy(a, b, scalar_done.at[i])
        for i, (a, b) in enumerate(
            [(targets_in, targets), (quarters_in, quarters), (rows_in, table_rows),
             (count_in, count)]
        )
    ]
    start_all(scalars)
    canvas[...] = jnp.zeros_like(canvas)
    coefficients[:, :, : table.shape[2]] = table[...]
    lane = lax.broadcasted_iota(jnp.int32, (1, side), 1).astype(f32)
    sub = lax.broadcasted_iota(jnp.int32, (8, side), 0).astype(f32)
    step = 8.0 / side
    wait_all(scalars)

    def add_group(j, carry):
        terms = []
        for member in range(group):
            n = group * j + member
            quarter = quarters[n]
            across = (lane + 0.5) / side - 1.0 + lax.rem(quarter, 2).astype(f32)
            down = (sub + 0.5 + top.astype(f32)) / side - 1.0 + (quarter // 2).astype(f32)
            entry = table_rows[n]
            chunk = coefficients[:, :, pl.ds(pl.multiple_of((entry // 128) * 128, 128), 128)]
            chunk = chunk.reshape(-1, 128)
            chunk = pltpu.roll(chunk, lax.rem(128 - lax.rem(entry, 128), 128), 1)
            poly = jnp.broadcast_to(chunk[:, :1], (chunk.shape[0], side))
            poly = [poly[i * nbasis : (i + 1) * nbasis] for i in range(chunk.shape[0] // nbasis)]
            constant = poly[0] + across * (poly[1] + across * poly[3])
            linear = poly[2] + across * poly[4]
            terms.append((constant, linear, poly[5], down))
        left = col_band[:, pl.ds(top, rows), :].reshape(nbasis * rows, 2 * side)
        halves = []
        for pair in range(group // 2):
            n = group * j + 2 * pair
            both = jnp.concatenate([pixels[n], pixels[n + 1]], axis=1)
            right = jnp.concatenate(split_right(both), axis=0)
            convolved = jnp.dot(left, right, preferred_element_type=f32)
            halves.append(split_left(convolved))
        for k in range(nbasis):
            at = slice(k * rows, (k + 1) * rows)
            stacked = []
            for member in range(group):
                first, second = halves[member // 2]
                lanes = slice((member % 2) * side, (member % 2 + 1) * side)
                stacked.append(jnp.concatenate([first[at, lanes], second[at, lanes]], axis=1))
            spread = jnp.dot(
                jnp.concatenate(stacked, axis=0), row_band[k], preferred_element_type=f32
            )
            for member in range(group):
                constant, linear, square, down = terms[member]
                b, d = linear[k : k + 1], square[k : k + 1]
                weight = constant[k : k + 1] + down * (b + down * d)
                change = step * b + d * (2.0 * step * down + step * step)
                second_change = (2.0 * step * step) * d
                for i in range(rows // 8):
                    value = weight * spread[member * rows + 8 * i : member * rows + 8 * i + 8]
                    if k == 0:
                        total[member, 8 * i : 8 * i + 8] = value
                    else:
                        total[member, 8 * i : 8 * i + 8] += value
                    if i < rows // 8 - 1:
                        weight = weight + change
                        change = change + second_change
        for member in range(group):
            n = group * j + member
            live = jnp.where(n < count[0], 1.0, 0.0).astype(f32)
            core, depth, down, across = place_of(where, targets[n], quarters[n])
            column = pl.ds(pl.multiple_of(across * side, side), side)
            canvas[core, down, depth, :, column] += (
                live / variance[n, pl.ds(top, rows), :]
            ) * total[member]
        return carry

    lax.fori_loop(0, blocks // group, add_group, 0)
    outs = [
        pltpu.make_async_copy(canvas.at[1], send_out, out_done.at[0]),
        pltpu.make_async_copy(canvas.at[0], keep_out, out_done.at[1]),
    ]
    start_all(outs)
    wait_all(outs)


def match(
    offset, rows, targets, quarters, table_rows, count, pixels, variance, table,
    col_band, row_band, depths,
):
    blocks, side, _ = pixels.shape
    nbasis = col_band.shape[0]
    group = min(blocks, GROUP_ROWS // rows)
    part = jax.ShapeDtypeStruct((2, depths, rows, 2 * side), f32)
    anywhere = pl.BlockSpec(memory_space=pltpu.HBM)
    vector = pl.BlockSpec(memory_space=pltpu.VMEM)
    entries = -(-table.shape[2] // 128) * 128
    scalars = (targets, quarters, table_rows, count)
    return pl.pallas_call(
        functools.partial(match_kernel, offset),
        out_shape=(part, part),
        in_specs=[anywhere] * 4 + [vector] * 5,
        out_specs=[anywhere] * 2,
        scratch_shapes=[pltpu.SMEM(a.shape, jnp.int32) for a in scalars]
        + [
            pltpu.VMEM((2, 2, depths, rows, 2 * side), f32),
            pltpu.VMEM((group, rows, side), f32),
            pltpu.VMEM(table.shape[:2] + (entries,), f32),
            pltpu.SemaphoreType.DMA((4,)),
            pltpu.SemaphoreType.DMA((2,)),
        ],
        compiler_params=pltpu.CompilerParams(vmem_limit_bytes=VMEM_BYTES),
        cost_estimate=pl.CostEstimate(
            flops=blocks * rows * side * 40960, bytes_accessed=10**7, transcendentals=0
        ),
    )(*scalars, pixels, variance, table, col_band, row_band)


def on_device(
    image, variance, dest_patch, quadrant, coef_index, block_count, coef_table, row_taps, col_taps
):
    pixels = image[0, 0]
    variances = variance[0, 0]
    targets = dest_patch[0, 0]
    quarters = quadrant[0, 0]
    table_rows = coef_index[0, 0]
    count = block_count[0]
    owners = lax.axis_size("patch")
    visits = lax.axis_size("visit")
    depths = owners // 2
    side = pixels.shape[1]
    half = side // 2
    table = jnp.transpose(coef_table, (2, 1, 0))
    together = lax.optimization_barrier

    def over_core(value):
        return lax.ppermute(value, "patch", [(i, i ^ 1) for i in range(owners)])

    def over_visit(value, flip):
        return lax.ppermute(value, "visit", [(i, i ^ flip) for i in range(visits)])

    def over_depth(value, shift):
        if depths & (depths - 1) == 0:
            pairs = [(i, i ^ (2 * shift)) for i in range(owners)]
        else:
            pairs = [(i, (i + 2 * shift) % owners) for i in range(owners)]
        return lax.ppermute(value, "patch", pairs)

    def pieces_of(value):
        order = [depths - 1] + list(range(1, depths - 1))
        return [over_depth(value[s], s) for s in order]

    def run(offset, rows, bands):
        return match(
            offset, rows, targets, quarters, table_rows, count, pixels, variances,
            table, bands[0], bands[1], depths,
        )

    def over_core_parts(value):
        return [over_core(value[y]) for y in range(2)]

    bands = make_bands(row_taps, col_taps, side)
    variances, bands = together((variances, bands))
    keep, send = sum_weights(targets, quarters, count, variances, depths)
    got = over_core(send)
    keep, bands = together((keep, bands))
    keep_far, send_far = run((1, 0), half, bands)
    got_far = over_core_parts(send_far)
    far = keep_far + jnp.stack(got_far)
    far, got = together((far, got))
    far_x = over_visit(far, 1)
    weight_odd, weights = keep[1] + got[1], keep[0] + got[0]
    far, weight_odd, weights, bands = together((far, weight_odd, weights, bands))
    weight_depth = over_depth(weight_odd, 1)
    keep_near, send_near = run((0, 0), half, bands)
    got_near = over_core_parts(send_near)
    keep_near, far_x = together((keep_near, far_x))
    near = [keep_near[y] + far_x[y] for y in range(2)]
    near, got_near = together((near, got_near))
    near = [near[y] + got_near[y] for y in range(2)]
    near_y = over_visit(near[1], 2)
    weights = [weights[x] + weight_depth[x] for x in range(2)]
    weight_x = over_visit(weights[1], 1)
    weight_own, near_own = together((weights[0], near[0]))
    weights = [weight_own[y] + weight_x[y] for y in range(2)]
    weight_y = over_visit(weights[1], 2)
    part = near_own + near_y
    pieces = pieces_of(part)
    weight_own, part = together((weights[0], part))
    weights = weight_own + weight_y
    weight_pieces = [over_depth(weights[s], 2 * s) for s in range(1, depths // 2)]
    weighted_sum = functools.reduce(jnp.add, pieces, part[0])
    weighted_sum, weights = together((weighted_sum, weights))
    weight_sum = functools.reduce(jnp.add, weight_pieces, weights[0])
    return weighted_sum[None], weight_sum[None]


def solution(mesh):
    placed = (
        P("visit", "patch", None, None, None),
        P("visit", "patch", None, None, None),
        P("visit", "patch", None),
        P("visit", "patch", None),
        P("visit", "patch", None),
        P("visit", "patch"),
        P(),
        P(),
        P(),
    )
    return jax.shard_map(
        on_device,
        mesh=mesh,
        in_specs=placed,
        out_specs=(P("patch", "visit", None), P("patch", "visit", None)),
        check_vma=False,
    )
```

```python
import functools

import jax
import jax.numpy as jnp
from jax import lax
from jax.experimental import pallas as pl
from jax.experimental.pallas import tpu as pltpu
from jax.sharding import PartitionSpec as P

f32 = jnp.float32
bf16 = jnp.bfloat16

SHARE = 1.0 / 32.0
KEEP = 1.0 - SHARE
VMEM_BYTES = 40 * 2**20
GROUP_ROWS = 1024


def split_left(value):
    first = value.astype(bf16)
    return first, (value - KEEP * first.astype(f32)).astype(bf16)


def split_right(value):
    first = (KEEP * value).astype(bf16)
    return first, ((value - first.astype(f32)) * (1.0 / SHARE)).astype(bf16)


def relative(depth, own, depths):
    if depths & (depths - 1) == 0:
        return depth ^ own
    return lax.rem(depth - own + depths, depths)


def my_place(depths):
    patch_at = lax.axis_index("patch")
    visit_at = lax.axis_index("visit")
    return lax.rem(patch_at, 2), patch_at // 2, depths, visit_at // 2, lax.rem(visit_at, 2)


def place_of(where, target, quarter):
    core = lax.rem(target, 2) ^ where[0]
    depth = relative(target // 2, where[1], where[2])
    return core, depth, (quarter // 2) ^ where[3], lax.rem(quarter, 2)


def start_all(copies):
    for copy in copies:
        copy.start()


def wait_all(copies):
    for copy in copies:
        copy.wait()


def weight_kernel(
    targets_in, quarters_in, count_in, variance, keep_out, send_out,
    targets, quarters, count, canvas, scalar_done,
):
    blocks, side, _ = variance.shape
    half = side // 2
    scalars = [
        pltpu.make_async_copy(a, b, scalar_done.at[i])
        for i, (a, b) in enumerate(
            [(targets_in, targets), (quarters_in, quarters), (count_in, count)]
        )
    ]
    start_all(scalars)
    canvas[...] = jnp.zeros_like(canvas)
    where = my_place(2 * canvas.shape[4])
    wait_all(scalars)

    def add_block(n, carry):
        live = jnp.where(n < count[0], 1.0, 0.0).astype(f32)
        inverse = live / variance[n]
        core, depth, down, across = place_of(where, targets[n], quarters[n])
        column = pl.ds(pl.multiple_of(across * side, side), side)
        for part in range(2):
            canvas[
                core, lax.rem(depth, 2), part ^ where[4], down, depth // 2, :, column
            ] += inverse[
                part * half : (part + 1) * half
            ]
        return carry

    lax.fori_loop(0, blocks, add_block, 0, unroll=4)
    send_out[...] = canvas[1]
    keep_out[...] = canvas[0]


def sum_weights(targets, quarters, count, variance, depths):
    blocks, side, _ = variance.shape
    half = side // 2
    part = jax.ShapeDtypeStruct((2, 2, 2, depths // 2, half, 2 * side), f32)
    anywhere = pl.BlockSpec(memory_space=pltpu.HBM)
    return pl.pallas_call(
        weight_kernel,
        out_shape=(part, part),
        in_specs=[anywhere] * 3 + [pl.BlockSpec(memory_space=pltpu.VMEM)],
        out_specs=[pl.BlockSpec(memory_space=pltpu.VMEM)] * 2,
        scratch_shapes=[
            pltpu.SMEM(targets.shape, jnp.int32),
            pltpu.SMEM(quarters.shape, jnp.int32),
            pltpu.SMEM(count.shape, jnp.int32),
            pltpu.VMEM((2,) + part.shape, f32),
            pltpu.SemaphoreType.DMA((3,)),
        ],
        compiler_params=pltpu.CompilerParams(vmem_limit_bytes=VMEM_BYTES),
        cost_estimate=pl.CostEstimate(flops=10**9, bytes_accessed=0, transcendentals=0),
    )(targets, quarters, count, variance)


def band_kernel(
    taps_in, col_band, row_band, row_padded, col_padded
):
    nbasis, taps = row_padded.shape[0], taps_in.shape[1]
    side = row_padded.shape[1]
    radius = (taps - 1) // 2
    row_padded[...] = jnp.zeros_like(row_padded)
    col_padded[...] = jnp.zeros_like(col_padded)
    row_padded[:, :taps] = taps_in[:nbasis]
    col_padded[:, :taps] = taps_in[nbasis:]
    row = lax.broadcasted_iota(jnp.int32, (side, side), 0)
    column = lax.broadcasted_iota(jnp.int32, (side, side), 1)
    near = jnp.abs(row - column) <= radius
    row_placed = pltpu.roll(row_padded[...], side - radius, 1)
    turn = (lax.rem(column - radius + row + side, side) == 0).astype(f32)
    col_placed = jnp.dot(
        col_padded[...], turn, precision=lax.Precision.HIGHEST, preferred_element_type=f32
    )
    for k in range(nbasis):
        base = jnp.broadcast_to(col_placed[k : k + 1], (side, side))
        band = jnp.where(near, pltpu.roll(base, 0, 1, stride=1, stride_axis=0), 0.0)
        first, second = split_left(band)
        col_band[k, :, :side] = first
        col_band[k, :, side:] = second
    for k in range(nbasis):
        base = jnp.broadcast_to(row_placed[k : k + 1], (side, side))
        band = jnp.where(near, pltpu.roll(base, 0, 1, stride=1, stride_axis=0), 0.0)
        first, second = split_right(band)
        row_band[k, :side, :] = first
        row_band[k, side:, :] = second


def make_bands(row_taps, col_taps, side):
    nbasis, taps = row_taps.shape
    vector = pl.BlockSpec(memory_space=pltpu.VMEM)
    col_shape, row_shape = (nbasis, side, 2 * side), (nbasis, 2 * side, side)
    tap_block = pl.BlockSpec((2 * nbasis, taps), lambda i: (0, 0))
    return pl.pallas_call(
        band_kernel,
        grid=(1,),
        out_shape=(
            jax.ShapeDtypeStruct(col_shape, bf16),
            jax.ShapeDtypeStruct(row_shape, bf16),
        ),
        in_specs=[tap_block],
        out_specs=[vector] * 2,
        scratch_shapes=[
            pltpu.VMEM((nbasis, side), f32),
            pltpu.VMEM((nbasis, side), f32),
        ],
        compiler_params=pltpu.CompilerParams(vmem_limit_bytes=VMEM_BYTES),
        cost_estimate=pl.CostEstimate(flops=10**9, bytes_accessed=0, transcendentals=0),
    )(jnp.concatenate([row_taps, col_taps], axis=0))


def match_kernel(
    offset, targets_in, quarters_in, rows_in, count_in, pixels, variance, table,
    col_band, row_band, keep_out, send_out,
    targets, quarters, table_rows, count, canvas, total, coefficients, scalar_done,
):
    side = pixels.shape[1]
    nbasis = col_band.shape[0]
    blocks = pixels.shape[0]
    group, rows, _ = total.shape
    far, start = offset
    where = my_place(canvas.shape[2])
    top = pl.multiple_of((where[4] ^ far) * (side // 2) + start, rows)
    scalars = [
        pltpu.make_async_copy(a, b, scalar_done.at[i])
        for i, (a, b) in enumerate(
            [(targets_in, targets), (quarters_in, quarters), (rows_in, table_rows),
             (count_in, count)]
        )
    ]
    start_all(scalars)
    canvas[...] = jnp.zeros_like(canvas)
    coefficients[:, :, : table.shape[2]] = table[...]
    lane = lax.broadcasted_iota(jnp.int32, (1, side), 1).astype(f32)
    sub = lax.broadcasted_iota(jnp.int32, (8, side), 0).astype(f32)
    step = 8.0 / side
    wait_all(scalars)

    def add_group(j, carry):
        terms = []
        for member in range(group):
            n = group * j + member
            quarter = quarters[n]
            across = (lane + 0.5) / side - 1.0 + lax.rem(quarter, 2).astype(f32)
            down = (sub + 0.5 + top.astype(f32)) / side - 1.0 + (quarter // 2).astype(f32)
            entry = table_rows[n]
            chunk = coefficients[:, :, pl.ds(pl.multiple_of((entry // 128) * 128, 128), 128)]
            chunk = chunk.reshape(-1, 128)
            chunk = pltpu.roll(chunk, lax.rem(128 - lax.rem(entry, 128), 128), 1)
            poly = jnp.broadcast_to(chunk[:, :1], (chunk.shape[0], side))
            poly = [poly[i * nbasis : (i + 1) * nbasis] for i in range(chunk.shape[0] // nbasis)]
            constant = poly[0] + across * (poly[1] + across * poly[3])
            linear = poly[2] + across * poly[4]
            terms.append((constant, linear, poly[5], down))
        left = col_band[:, pl.ds(top, rows), :].reshape(nbasis * rows, 2 * side)
        halves = []
        for pair in range(group // 2):
            n = group * j + 2 * pair
            both = jnp.concatenate([pixels[n], pixels[n + 1]], axis=1)
            right = jnp.concatenate(split_right(both), axis=0)
            convolved = jnp.dot(left, right, preferred_element_type=f32)
            halves.append(split_left(convolved))
        for k in range(nbasis):
            at = slice(k * rows, (k + 1) * rows)
            stacked = []
            for member in range(group):
                first, second = halves[member // 2]
                lanes = slice((member % 2) * side, (member % 2 + 1) * side)
                stacked.append(jnp.concatenate([first[at, lanes], second[at, lanes]], axis=1))
            spread = jnp.dot(
                jnp.concatenate(stacked, axis=0), row_band[k], preferred_element_type=f32
            )
            for member in range(group):
                constant, linear, square, down = terms[member]
                b, d = linear[k : k + 1], square[k : k + 1]
                weight = constant[k : k + 1] + down * (b + down * d)
                change = step * b + d * (2.0 * step * down + step * step)
                second_change = (2.0 * step * step) * d
                for i in range(rows // 8):
                    value = weight * spread[member * rows + 8 * i : member * rows + 8 * i + 8]
                    if k == 0:
                        total[member, 8 * i : 8 * i + 8] = value
                    else:
                        total[member, 8 * i : 8 * i + 8] += value
                    if i < rows // 8 - 1:
                        weight = weight + change
                        change = change + second_change
        for member in range(group):
            n = group * j + member
            live = jnp.where(n < count[0], 1.0, 0.0).astype(f32)
            core, depth, down, across = place_of(where, targets[n], quarters[n])
            column = pl.ds(pl.multiple_of(across * side, side), side)
            canvas[core, down, depth, :, column] += (
                live / variance[n, pl.ds(top, rows), :]
            ) * total[member]
        return carry

    lax.fori_loop(0, blocks // group, add_group, 0)
    send_out[...] = canvas[1]
    keep_out[...] = canvas[0]


def match(
    offset, rows, targets, quarters, table_rows, count, pixels, variance, table,
    col_band, row_band, depths,
):
    blocks, side, _ = pixels.shape
    nbasis = col_band.shape[0]
    group = min(blocks, GROUP_ROWS // rows)
    part = jax.ShapeDtypeStruct((2, depths, rows, 2 * side), f32)
    anywhere = pl.BlockSpec(memory_space=pltpu.HBM)
    vector = pl.BlockSpec(memory_space=pltpu.VMEM)
    entries = -(-table.shape[2] // 128) * 128
    scalars = (targets, quarters, table_rows, count)
    return pl.pallas_call(
        functools.partial(match_kernel, offset),
        out_shape=(part, part),
        in_specs=[anywhere] * 4 + [vector] * 5,
        out_specs=[vector] * 2,
        scratch_shapes=[pltpu.SMEM(a.shape, jnp.int32) for a in scalars]
        + [
            pltpu.VMEM((2, 2, depths, rows, 2 * side), f32),
            pltpu.VMEM((group, rows, side), f32),
            pltpu.VMEM(table.shape[:2] + (entries,), f32),
            pltpu.SemaphoreType.DMA((4,)),
        ],
        compiler_params=pltpu.CompilerParams(vmem_limit_bytes=VMEM_BYTES),
        cost_estimate=pl.CostEstimate(
            flops=blocks * rows * side * 40960, bytes_accessed=10**7, transcendentals=0
        ),
    )(*scalars, pixels, variance, table, col_band, row_band)


def on_device(
    image, variance, dest_patch, quadrant, coef_index, block_count, coef_table, row_taps, col_taps
):
    pixels = image[0, 0]
    variances = variance[0, 0]
    targets = dest_patch[0, 0]
    quarters = quadrant[0, 0]
    table_rows = coef_index[0, 0]
    count = block_count[0]
    owners = lax.axis_size("patch")
    visits = lax.axis_size("visit")
    depths = owners // 2
    side = pixels.shape[1]
    half = side // 2
    table = jnp.transpose(coef_table, (2, 1, 0))
    together = lax.optimization_barrier

    def over_core(value):
        return lax.ppermute(value, "patch", [(i, i ^ 1) for i in range(owners)])

    def over_visit(value, flip):
        return lax.ppermute(value, "visit", [(i, i ^ flip) for i in range(visits)])

    def over_depth(value, shift):
        if depths & (depths - 1) == 0:
            pairs = [(i, i ^ (2 * shift)) for i in range(owners)]
        else:
            pairs = [(i, (i + 2 * shift) % owners) for i in range(owners)]
        return lax.ppermute(value, "patch", pairs)

    def pieces_of(value):
        order = [depths - 1] + list(range(1, depths - 1))
        return [over_depth(value[s], s) for s in order]

    def run(offset, rows, bands):
        return match(
            offset, rows, targets, quarters, table_rows, count, pixels, variances,
            table, bands[0], bands[1], depths,
        )

    def over_core_parts(value):
        return [over_core(value[y]) for y in range(2)]

    bands = make_bands(row_taps, col_taps, side)
    variances, bands = together((variances, bands))
    keep, send = sum_weights(targets, quarters, count, variances, depths)
    got = over_core(send)
    keep, bands = together((keep, bands))
    keep_far, send_far = run((1, 0), half, bands)
    got_far = over_core_parts(send_far)
    far = keep_far + jnp.stack(got_far)
    far, got = together((far, got))
    far_x = over_visit(far, 1)
    weight_odd, weights = keep[1] + got[1], keep[0] + got[0]
    far, weight_odd, weights, bands = together((far, weight_odd, weights, bands))
    weight_depth = over_depth(weight_odd, 1)
    keep_near, send_near = run((0, 0), half, bands)
    got_near = over_core_parts(send_near)
    keep_near, far_x = together((keep_near, far_x))
    near = [keep_near[y] + far_x[y] for y in range(2)]
    near, got_near = together((near, got_near))
    near = [near[y] + got_near[y] for y in range(2)]
    near_y = over_visit(near[1], 2)
    weights = [weights[x] + weight_depth[x] for x in range(2)]
    weight_x = over_visit(weights[1], 1)
    weight_own, near_own = together((weights[0], near[0]))
    weights = [weight_own[y] + weight_x[y] for y in range(2)]
    weight_y = over_visit(weights[1], 2)
    part = near_own + near_y
    pieces = pieces_of(part)
    weight_own, part = together((weights[0], part))
    weights = weight_own + weight_y
    weight_pieces = [over_depth(weights[s], 2 * s) for s in range(1, depths // 2)]
    weighted_sum = functools.reduce(jnp.add, pieces, part[0])
    weighted_sum, weights = together((weighted_sum, weights))
    weight_sum = functools.reduce(jnp.add, weight_pieces, weights[0])
    return weighted_sum[None], weight_sum[None]


def solution(mesh):
    placed = (
        P("visit", "patch", None, None, None),
        P("visit", "patch", None, None, None),
        P("visit", "patch", None),
        P("visit", "patch", None),
        P("visit", "patch", None),
        P("visit", "patch"),
        P(),
        P(),
        P(),
    )
    return jax.shard_map(
        on_device,
        mesh=mesh,
        in_specs=placed,
        out_specs=(P("patch", "visit", None), P("patch", "visit", None)),
        check_vma=False,
    )
```
